32 devices in a mesh: gx: 4 (over x, core), gy: 2 (over y), gz: 4 (over z).
Axes of the slice: x: 2, y: 2, z: 4, core: 2. Of those that a mesh axis runs over, the one named last changes fastest.
Arguments:
- phase: int32 [256, 16, 512], P('gx', 'gy', 'gz'), may hold values from 0 to 2
- perm_scale: float32 [256, 16, 512], P('gx', 'gy', 'gz'), may hold values from 0.5 to 2
- magnetization: bfloat16 [3, 256, 16, 512], P(None, 'gx', 'gy', 'gz'), may hold values from -4 to 4
- stiffness: float32 [256, 16, 512], P(('gx', 'gy'), None, 'gz'), may hold values from 0.5 to 4
Outputs:
- strain: bfloat16 [6, 256, 16, 512], P(None, 'gx', 'gy', 'gz')
The draws below stay inside these ranges and needn't reach their ends.
All inputs are finite; a program needn't handle non-finite values.
Results may differ from the reference program's by a relative error of at most 0.001.
The reference program's roundings to bfloat16 on the way (of `moments` and `force`) count: a program that leaves them out, or rounds other values in their place, can miss the bound.
Values may be sent and summed in bfloat16 or wider, within the bound.
A program may use at most 64 MiB of HBM per device.

```python
import math
import jax
import jax.numpy as jnp
from jax import lax

SWEEPS = 3
NX = 256
NY = 16
NZ = 512


def touch_ends(array, key, low, top_value):
    longest = array.shape.index(max(array.shape))
    spots = []
    for shift in (0, 1):
        where = [jax.random.randint(jax.random.fold_in(key, axis), (), 0, length) for axis, length in enumerate(array.shape)]
        where[longest] = (where[longest] + shift) % array.shape[longest]
        spots.append(tuple(where))
    return array.at[spots[0]].set(low).at[spots[1]].set(top_value)


def levels(rng, shape, pieces, least, largest):
    loudness, own = 1.0, jax.random.fold_in(rng, 6)
    for position, blocks in pieces:
        steps = jnp.exp(jax.random.uniform(jax.random.fold_in(own, position), (blocks,), jnp.float32, least / len(pieces), largest / len(pieces)))
        loudness = loudness * jnp.repeat(steps, shape[position] // blocks).reshape([-1 if axis == position else 1 for axis in range(len(shape))])
    return loudness


def centred(stream_key, dims, spread, reach, pieces=(), held_as=jnp.bfloat16):
    values = jax.random.normal(stream_key, dims, jnp.float32) * spread
    if len(pieces) > 0:
        values = levels(stream_key, dims, pieces, -0.22, 0.18) * values
    return jnp.clip(values, min=-reach, max=reach).astype(held_as)


def setup_inputs(seed: int = 0) -> dict:
    key_of = jax.random.split(jax.random.key(seed), 5)
    return {
        "phase": touch_ends(jax.random.randint(key_of[0], (NX, NY, NZ), 0, 3), jax.random.fold_in(key_of[0], 1), 0, 2).astype(jnp.int32),
        "perm_scale": jnp.clip(jnp.exp(math.log(2.0) - 1.3862944 * jax.random.uniform(key_of[1], (NX, NY, NZ), jnp.float32) ** levels(key_of[1], (NX, NY, NZ), ((0, 4), (1, 2), (2, 4)), -0.2, 0.2)), 0.5, 2.0),
        "magnetization": centred(key_of[2], (3, NX, NY, NZ), 1.0, 4.0, ((1, 4), (2, 2), (3, 4))),
        "stiffness": jnp.clip(jnp.exp(math.log(4.0) - 2.0794415 * jax.random.uniform(key_of[3], (NX, NY, NZ), jnp.float32) ** levels(key_of[3], (NX, NY, NZ), ((0, 8), (2, 4)), -0.2, 0.2)), 0.5, 4.0),
    }


STRAIN_PAIRS = ((0, 0), (1, 1), (2, 2), (0, 1), (1, 2), (0, 2))
MAGNETO = 4.0


def chebyshev_weights(middle, radius, count):
    return [1.0 / (middle + radius * math.cos((2 * counter + 1) * math.pi / (2 * count))) for counter in range(count)]


def unit_offset(dimension, sign):
    offsets = [0, 0, 0]
    offsets[dimension] = sign
    return offsets


def window(padded, offsets):
    shape = padded.shape[-3:]
    selection = tuple(slice(1 + moved, extent - 1 + moved) for moved, extent in zip(offsets, shape))
    leading = tuple(slice(None) for counter in range(padded.ndim - 3))
    return padded[leading + selection]


def central(padded, dimension):
    return (window(padded, unit_offset(dimension, 1)) - window(padded, unit_offset(dimension, -1))) * 0.5


def neighbours(padded):
    total = window(padded, unit_offset(0, 1)) + window(padded, unit_offset(0, -1))
    for dimension in (1, 2):
        total = total + window(padded, unit_offset(dimension, 1)) + window(padded, unit_offset(dimension, -1))
    return total


def magnet_force(moments_pad, potential_pad):
    total = [moments_pad[dimension] - central(potential_pad, dimension) for dimension in range(3)]
    inner = moments_pad[0] * total[0] + moments_pad[1] * total[1] + moments_pad[2] * total[2]
    stress = {}
    for first, second in STRAIN_PAIRS:
        value = 0.5 * (moments_pad[first] * total[second] + moments_pad[second] * total[first])
        if first == second:
            value = value - inner / 3.0
        stress[(first, second)] = MAGNETO * value
        stress[(second, first)] = stress[(first, second)]
    force = []
    for first in range(3):
        acc = central(stress[(first, 0)], 0)
        for second in (1, 2):
            acc = acc + central(stress[(first, second)], second)
        force.append(acc)
    return jnp.stack(force)


def navier(padded):
    result = []
    for first in range(3):
        center = window(padded[first], [0, 0, 0])
        value = 6.0 * center - neighbours(padded[first])
        second_diff = window(padded[first], unit_offset(first, 1)) - 2.0 * center + window(padded[first], unit_offset(first, -1))
        for second in range(3):
            if second != first:
                plus_plus = [0, 0, 0]
                plus_plus[first] = 1
                plus_plus[second] = 1
                plus_minus = [0, 0, 0]
                plus_minus[first] = 1
                plus_minus[second] = -1
                minus_plus = [0, 0, 0]
                minus_plus[first] = -1
                minus_plus[second] = 1
                minus_minus = [0, 0, 0]
                minus_minus[first] = -1
                minus_minus[second] = -1
                second_diff = second_diff + 0.25 * (window(padded[second], plus_plus) - window(padded[second], plus_minus) - window(padded[second], minus_plus) + window(padded[second], minus_minus))
        result.append(value - second_diff)
    return jnp.stack(result)


def strain_from(padded):
    result = []
    for first, second in STRAIN_PAIRS:
        result.append(0.5 * (central(padded[second], first) + central(padded[first], second)))
    return jnp.stack(result)


def pad_vector(field):
    return jnp.pad(field, ((0, 0), (1, 1), (1, 1), (1, 1)))


def reference(phase, perm_scale, magnetization, stiffness):
    magnetic = phase == 0
    permeability = jnp.where(magnetic, 4.0, jnp.where(phase == 1, 1.5, 1.0)).astype(jnp.float32) * perm_scale
    moments = (magnetization * magnetic.astype(jnp.bfloat16)[None]).astype(jnp.float32)
    moments_pad = pad_vector(moments)
    source = -(central(moments_pad[0], 0) + central(moments_pad[1], 1) + central(moments_pad[2], 2))
    weights = chebyshev_weights(1.0, 0.9, SWEEPS)
    diagonal = 6.0 * permeability
    potential = weights[0] * source / diagonal
    for counter in range(1, SWEEPS):
        padded = jnp.pad(potential, 1)
        potential = potential + weights[counter] * (source - permeability * (6.0 * potential - neighbours(padded))) / diagonal
    force = magnet_force(moments_pad, jnp.pad(potential, 2)).astype(jnp.bfloat16)
    load = lax.optimization_barrier(force).astype(jnp.float32)
    elastic_weights = chebyshev_weights(1.3, 1.2, SWEEPS)
    elastic_diag = 8.0 * stiffness
    displacement = elastic_weights[0] * load / elastic_diag
    for counter in range(1, SWEEPS):
        padded = pad_vector(displacement)
        displacement = displacement + elastic_weights[counter] * (load - stiffness * navier(padded)) / elastic_diag
    return strain_from(pad_vector(displacement)).astype(jnp.bfloat16)
```

```python
import functools
import math

import jax
import jax.numpy as jnp
from jax import lax
from jax.experimental import pallas as pl
from jax.experimental.pallas import tpu as pltpu
from jax.sharding import PartitionSpec as P

SWEEPS = 3
STRAIN_PAIRS = ((0, 0), (1, 1), (2, 2), (0, 1), (1, 2), (0, 2))
STRESS_AT = {(0, 0): 0, (1, 1): 1, (2, 2): 2, (0, 1): 3, (1, 0): 3, (1, 2): 4, (2, 1): 4, (0, 2): 5, (2, 0): 5}
MAGNETO = 4.0
MESH = pl.DeviceIdType.MESH
RIM = 4


def chebyshev_weights(middle, radius, count):
    return [
        1.0 / (middle + radius * math.cos((2 * counter + 1) * math.pi / (2 * count)))
        for counter in range(count)
    ]


def shift(value, dimension, step):
    size = value.shape[dimension]
    return pltpu.roll(value, (-step) % size, dimension)


def sides(value, dimension):
    return shift(value, dimension, 1), shift(value, dimension, -1)


def kernel(sizes, phase, perm, magnet, stiff, out, flat, diag, mom, src, pot1, pot2, stress, load, disp1, disp2,
           mask, modulus, rx_m, rx_s, rx_g, tz_m, tz_s, tz_g, rz_m, rz_s, rz_g, send_sem, recv_sem, g_send, g_recv, g_local):
    nx, ny, nz, X, Y, Z = sizes
    XR, ZR = X + 2 * RIM, 2 * Z
    gx, gy, gz = lax.axis_index("gx"), lax.axis_index("gy"), lax.axis_index("gz")
    place = {"gx": gx, "gy": gy, "gz": gz}
    count = {"gx": nx, "gy": ny, "gz": nz}

    def has(axis, side):
        return place[axis] > 0 if side == 0 else place[axis] < count[axis] - 1

    def device(axis, index):
        at = dict(place)
        at[axis] = index
        return (at["gx"], at["gy"], at["gz"])

    def beside(axis, side):
        return device(axis, place[axis] + (-1 if side == 0 else 1))

    barrier = pltpu.get_barrier_semaphore()
    greeted = 0
    for axis in ("gx", "gz"):
        for side in (0, 1):
            @pl.when(has(axis, side))
            def _():
                pl.semaphore_signal(barrier, inc=1, device_id=beside(axis, side), device_id_type=MESH)
            greeted = greeted + has(axis, side).astype(jnp.int32)
    for k in range(1, ny):
        pl.semaphore_signal(barrier, inc=1, device_id=device("gy", lax.rem(gy + k, ny)), device_id_type=MESH)
    greeted = greeted + (ny - 1)

    for c in range(3):
        flat[c] = magnet[c].astype(jnp.float32)
    for y in range(Y):
        rows = pl.ds(y, X, stride=Y)
        kind = phase[rows, :]
        magnetic = kind == 0
        mu = jnp.where(magnetic, 4.0, jnp.where(kind == 1, 1.5, 1.0)).astype(jnp.float32) * perm[rows, :]
        diag[y] = 6.0 * mu
        for c in range(3):
            mom[c, RIM + y, 0:X, 0:Z] = jnp.where(magnetic, flat[c, rows, :], 0.0)

    row = lax.broadcasted_iota(jnp.int32, (XR, ZR), 0)
    lane = lax.broadcasted_iota(jnp.int32, (XR, ZR), 1)
    real = ((row < X) | ((row < X + RIM) & has("gx", 1)) | ((row >= X + RIM) & has("gx", 0))) & (
        (lane < Z) | ((lane < Z + Z // 2) & has("gz", 1)) | ((lane >= Z + Z // 2) & has("gz", 0)))
    mask[...] = jnp.where(real, 1.0, 0.0)

    for buffer in (rx_m, rx_s, rx_g):
        for side in (0, 1):
            @pl.when(jnp.logical_not(has("gx", side)))
            def _():
                buffer[side] = jnp.zeros(buffer.shape[1:], jnp.float32)
    for buffer in (rz_m, rz_s, rz_g):
        for side in (0, 1):
            @pl.when(jnp.logical_not(has("gz", side)))
            def _():
                buffer[side] = jnp.zeros(buffer.shape[1:], jnp.float32)
    for buffer in (mom, src, load):
        for side, first in ((0, 0), (1, RIM + Y)):
            @pl.when(jnp.logical_not(has("gy", side)))
            def _():
                for c in range(3 if buffer is not src else 1):
                    buffer[c, first:first + RIM] = jnp.zeros((RIM, XR, ZR), jnp.float32)

    pl.semaphore_wait(barrier, greeted)

    span = X // ny
    for k in range(1, ny):
        peer = lax.rem(gy + k, ny)
        pltpu.make_async_remote_copy(
            src_ref=stiff.at[:, pl.ds(pl.multiple_of(peer * Y, Y), Y), :],
            dst_ref=modulus.at[pl.ds(gy * span, span)],
            send_sem=g_send.at[k], recv_sem=g_recv.at[k],
            device_id=device("gy", peer), device_id_type=MESH).start()
    own = pltpu.make_async_copy(
        stiff.at[:, pl.ds(pl.multiple_of(gy * Y, Y), Y), :], modulus.at[pl.ds(gy * span, span)], g_local)
    own.start()

    def swap(axis, which, pairs):
        for side in (0, 1):
            @pl.when(has(axis, side))
            def _():
                pltpu.make_async_remote_copy(
                    src_ref=pairs[side][0], dst_ref=pairs[side][1], send_sem=send_sem.at[which, side],
                    recv_sem=recv_sem.at[which, 1 - side], device_id=beside(axis, side), device_id_type=MESH).start()
        for side in (0, 1):
            @pl.when(has(axis, side))
            def _():
                copy = pltpu.make_async_remote_copy(
                    src_ref=pairs[side][0], dst_ref=pairs[1 - side][1], send_sem=send_sem.at[which, side],
                    recv_sem=recv_sem.at[which, side], device_id=beside(axis, side), device_id_type=MESH)
                copy.wait_send()
                copy.wait_recv()

    block = lax.rem(lax.broadcasted_iota(jnp.int32, (XR, Z), 1) + RIM, Z) // (2 * RIM)
    from_after = lax.rem(lax.broadcasted_iota(jnp.int32, (XR, Z), 1), 2 * RIM) < RIM

    def exchange(buffer, parts, width, which, rx, tz, rz):
        own_planes = slice(RIM, RIM + Y)
        low, high = RIM - width, RIM + Y + width
        swap("gx", which, (
            (buffer.at[:, own_planes, 0:2 * RIM, 0:Z], rx.at[1]),
            (buffer.at[:, own_planes, X - 2 * RIM:X, 0:Z], rx.at[0])))
        upper = lax.broadcasted_iota(jnp.int32, (Y, 2 * RIM, Z), 1) < RIM
        for c in range(parts):
            buffer[c, own_planes, X:XR, 0:Z] = jnp.where(upper, rx[1, c], rx[0, c])
        swap("gy", which + 1, (
            (buffer.at[:, RIM:RIM + width, :, 0:Z], buffer.at[:, RIM + Y:high, :, 0:Z]),
            (buffer.at[:, RIM + Y - width:RIM + Y, :, 0:Z], buffer.at[:, low:RIM, :, 0:Z])))
        for c in range(parts):
            packed = jnp.zeros((XR, Z), jnp.float32)
            for y in range(low, high):
                packed = jnp.where(block == y, pltpu.roll(buffer[c, y, :, 0:Z], (2 * RIM * y) % Z, 1), packed)
            tz[c] = packed
        swap("gz", which + 2, ((tz, rz.at[1]), (tz, rz.at[0])))
        for c in range(parts):
            both = jnp.where(from_after, rz[1, c], rz[0, c])
            for y in range(low, high):
                buffer[c, y, :, Z:ZR] = pltpu.roll(both, (-2 * RIM * y) % Z, 1)

    def clear_outside(buffer, parts):
        for side, first in ((0, 0), (1, RIM + Y)):
            @pl.when(jnp.logical_not(has("gy", side)))
            def _():
                for c in range(parts):
                    buffer[c, first:first + RIM] = jnp.zeros((RIM, XR, ZR), jnp.float32)

    exchange(mom, 3, 1, 0, rx_m, tz_m, rz_m)

    @pl.loop(RIM, RIM + Y)
    def _(y):
        xp, xm = sides(mom[0, y], 0)
        zp, zm = sides(mom[2, y], 1)
        total = (xp - xm) + (mom[1, y + 1] - mom[1, y - 1]) + (zp - zm)
        src[0, y, 0:X, 0:Z] = -0.5 * total[0:X, 0:Z] / diag[y - RIM]

    exchange(src, 1, 4, 3, rx_s, tz_s, rz_s)
    w = chebyshev_weights(1.0, 0.9, SWEEPS)

    def neighbours(buffer, y):
        xp, xm = sides(buffer[0, y], 0)
        zp, zm = sides(buffer[0, y], 1)
        return xp + xm + buffer[0, y + 1] + buffer[0, y - 1] + zp + zm

    @pl.loop(1, 2 * RIM + Y - 1)
    def _(y):
        pot1[0, y] = mask[...] * ((w[0] + w[1] - w[0] * w[1]) * src[0, y] + (w[0] * w[1] / 6.0) * neighbours(src, y))

    clear_outside(pot1, 1)

    @pl.loop(2, 2 * RIM + Y - 2)
    def _(y):
        center = pot1[0, y]
        pot2[0, y] = mask[...] * (center + w[2] * (src[0, y] - center + neighbours(pot1, y) * (1.0 / 6.0)))

    clear_outside(pot2, 1)

    @pl.loop(RIM - 1, RIM + Y + 1)
    def _(y):
        center = pot2[0, y]
        xp, xm = sides(center, 0)
        zp, zm = sides(center, 1)
        m = [mom[c, y] for c in range(3)]
        grad = [xp - xm, pot2[0, y + 1] - pot2[0, y - 1], zp - zm]
        total = [m[c] - 0.5 * grad[c] for c in range(3)]
        inner = (m[0] * total[0] + m[1] * total[1] + m[2] * total[2]) / 3.0
        for number, (a, b) in enumerate(STRAIN_PAIRS):
            if a == b:
                value = MAGNETO * (m[a] * total[a] - inner)
            else:
                value = (0.5 * MAGNETO) * (m[a] * total[b] + m[b] * total[a])
            stress[number, y] = value

    for k in range(1, ny):
        peer = lax.rem(gy + k, ny)
        copy = pltpu.make_async_remote_copy(
            src_ref=stiff.at[:, pl.ds(pl.multiple_of(peer * Y, Y), Y), :],
            dst_ref=modulus.at[pl.ds(lax.rem(gy + ny - k, ny) * span, span)],
            send_sem=g_send.at[k], recv_sem=g_recv.at[k],
            device_id=device("gy", peer), device_id_type=MESH)
        copy.wait_send()
        copy.wait_recv()
    own.wait()
    for y in range(Y):
        diag[y] = 8.0 * modulus.reshape(X * Y, Z)[pl.ds(y, X, stride=Y), :]

    @pl.loop(RIM, RIM + Y)
    def _(y):
        for a in range(3):
            xp, xm = sides(stress[STRESS_AT[a, 0], y], 0)
            zp, zm = sides(stress[STRESS_AT[a, 2], y], 1)
            n = STRESS_AT[a, 1]
            force = 0.5 * ((xp - xm) + (stress[n, y + 1] - stress[n, y - 1]) + (zp - zm))[0:X, 0:Z]
            load[a, y, 0:X, 0:Z] = force.astype(jnp.bfloat16).astype(jnp.float32) / diag[y - RIM]

    exchange(load, 3, 3, 6, rx_g, tz_g, rz_g)
    v = chebyshev_weights(1.3, 1.2, SWEEPS)

    def navier(buffer, y):
        u = [buffer[c, y] for c in range(3)]
        up = [buffer[c, y + 1] for c in range(3)]
        um = [buffer[c, y - 1] for c in range(3)]
        xs = [sides(u[c], 0) for c in range(3)]
        zs = [sides(u[c], 1) for c in range(3)]
        dy = [up[c] - um[c] for c in range(3)]
        dx0 = xs[0][0] - xs[0][1]
        dz2 = zs[2][0] - zs[2][1]
        ap, am = sides(dy[1] + dz2, 0)
        bp, bm = sides(dy[0], 0)
        cp, cm = sides(dy[2], 1)
        ep, em = sides(dx0 + dy[1], 1)
        mixed = [ap - am, (bp - bm) + (cp - cm), ep - em]
        result = []
        for c in range(3):
            along = [xs[c][0] + xs[c][1], up[c] + um[c], zs[c][0] + zs[c][1]]
            rest = along[0] + along[1] + along[2] + along[c]
            result.append(8.0 * u[c] - rest - 0.25 * mixed[c])
        return u, result

    @pl.loop(2, 2 * RIM + Y - 2)
    def _(y):
        u, result = navier(load, y)
        for c in range(3):
            disp1[c, y] = mask[...] * ((v[0] + v[1]) * u[c] - (v[0] * v[1] / 8.0) * result[c])

    clear_outside(disp1, 3)

    @pl.loop(3, 2 * RIM + Y - 3)
    def _(y):
        u, result = navier(disp1, y)
        for c in range(3):
            disp2[c, y] = mask[...] * (u[c] + v[2] * (load[c, y] - 0.125 * result[c]))

    clear_outside(disp2, 3)

    for y in range(RIM, RIM + Y):
        rows = pl.ds(y - RIM, X, stride=Y)
        gradient = {}
        for c in range(3):
            u = disp2[c, y]
            xp, xm = sides(u, 0)
            zp, zm = sides(u, 1)
            gradient[c, 0] = (xp - xm)[0:X, 0:Z]
            gradient[c, 1] = (disp2[c, y + 1] - disp2[c, y - 1])[0:X, 0:Z]
            gradient[c, 2] = (zp - zm)[0:X, 0:Z]
        for number, (a, b) in enumerate(STRAIN_PAIRS):
            flat[number, rows, :] = 0.25 * (gradient[b, a] + gradient[a, b])
    for number in range(6):
        out[number] = flat[number].astype(jnp.bfloat16)


def per_device(phase, perm_scale, magnetization, stiffness):
    X, Y, Z = phase.shape
    nx, ny, nz = (lax.axis_size(axis) for axis in ("gx", "gy", "gz"))
    XR, ZR, P2 = X + 2 * RIM, 2 * Z, Y + 2 * RIM
    f32 = jnp.float32
    field = lambda parts: pltpu.VMEM((parts, P2, XR, ZR), f32)
    rx = lambda parts: pltpu.VMEM((2, parts, Y, 2 * RIM, Z), f32)
    vmem = pl.BlockSpec(memory_space=pltpu.VMEM)
    result = pl.pallas_call(
        functools.partial(kernel, (nx, ny, nz, X, Y, Z)),
        out_shape=jax.ShapeDtypeStruct((6, X * Y, Z), jnp.bfloat16),
        in_specs=[vmem] * 4,
        out_specs=vmem,
        scratch_shapes=[
            pltpu.VMEM((6, X * Y, Z), f32), pltpu.VMEM((Y, X, Z), f32),
            field(3), field(1), field(1), field(1), field(6), field(3), field(3), field(3),
            pltpu.VMEM((XR, ZR), f32), pltpu.VMEM((X, Y, Z), f32),
            rx(3), rx(1), rx(3),
            pltpu.VMEM((3, XR, Z), f32), pltpu.VMEM((1, XR, Z), f32), pltpu.VMEM((3, XR, Z), f32),
            pltpu.VMEM((2, 3, XR, Z), f32), pltpu.VMEM((2, 1, XR, Z), f32), pltpu.VMEM((2, 3, XR, Z), f32),
            pltpu.SemaphoreType.DMA((9, 2)), pltpu.SemaphoreType.DMA((9, 2)),
            pltpu.SemaphoreType.DMA((ny,)), pltpu.SemaphoreType.DMA((ny,)), pltpu.SemaphoreType.DMA,
        ],
        compiler_params=pltpu.CompilerParams(
            collective_id=0, has_side_effects=True, vmem_limit_bytes=48 * 1024 * 1024),
    )(phase.reshape(X * Y, Z), perm_scale.reshape(X * Y, Z), magnetization.reshape(3, X * Y, Z), stiffness)
    return result.reshape(6, X, Y, Z)


def solution(mesh):
    placed = (
        P("gx", "gy", "gz"),
        P("gx", "gy", "gz"),
        P(None, "gx", "gy", "gz"),
        P(("gx", "gy"), None, "gz"),
    )
    return jax.shard_map(
        per_device, mesh=mesh, in_specs=placed, out_specs=P(None, "gx", "gy", "gz"), check_vma=False
    )
```

```python
import functools
import math

import jax
import jax.numpy as jnp
from jax import lax
from jax.experimental import pallas as pl
from jax.experimental.pallas import tpu as pltpu
from jax.sharding import PartitionSpec as P

SWEEPS = 3
STRAIN_PAIRS = ((0, 0), (1, 1), (2, 2), (0, 1), (1, 2), (0, 2))
STRESS_AT = {(0, 0): 0, (1, 1): 1, (2, 2): 2, (0, 1): 3, (1, 0): 3, (1, 2): 4, (2, 1): 4, (0, 2): 5, (2, 0): 5}
MAGNETO = 4.0
MESH = pl.DeviceIdType.MESH
RIM = 4


def chebyshev_weights(middle, radius, count):
    return [
        1.0 / (middle + radius * math.cos((2 * counter + 1) * math.pi / (2 * count)))
        for counter in range(count)
    ]


def shift(value, dimension, step):
    size = value.shape[dimension]
    return pltpu.roll(value, (-step) % size, dimension)


def sides(value, dimension):
    return shift(value, dimension, 1), shift(value, dimension, -1)


def kernel(sizes, phase_in, perm_in, magnet_in, stiff, out, phase, perm, magnet, in_sem, flat, diag, mom, src, pot1, pot2, stress, load, disp1, disp2,
           mask, modulus, rx_m, rx_s, rx_g, tz_a, tz_m, tz_s, tz_g, rz_a, rz_m, rz_s, rz_g, send_sem, recv_sem, g_send, g_recv, g_local):
    nx, ny, nz, X, Y, Z = sizes
    XR, ZR = X + 2 * RIM, 2 * Z
    gx, gy, gz = lax.axis_index("gx"), lax.axis_index("gy"), lax.axis_index("gz")
    place = {"gx": gx, "gy": gy, "gz": gz}
    count = {"gx": nx, "gy": ny, "gz": nz}

    fetches = [pltpu.make_async_copy(a, b, in_sem.at[i]) for i, (a, b) in enumerate(
        ((magnet_in, magnet), (phase_in, phase), (perm_in, perm)))]
    for fetch in fetches:
        fetch.start()

    def has(axis, side):
        return place[axis] > 0 if side == 0 else place[axis] < count[axis] - 1

    def device(axis, index):
        at = dict(place)
        at[axis] = index
        return (at["gx"], at["gy"], at["gz"])

    def exists(step):
        there = None
        for axis, move in zip(("gx", "gy", "gz"), step):
            if move:
                this = has(axis, 0 if move < 0 else 1)
                there = this if there is None else there & this
        return there

    def beside(step):
        return (gx + step[0], gy + step[1], gz + step[2])

    barrier = pltpu.get_barrier_semaphore()
    greeted = 0
    diagonals = [(dx, dy, 0) for dx in (-1, 1) for dy in (-1, 1)]
    for step in [(-1, 0, 0), (1, 0, 0), (0, 0, -1), (0, 0, 1)] + diagonals:
        @pl.when(exists(step))
        def _():
            pl.semaphore_signal(barrier, inc=1, device_id=beside(step), device_id_type=MESH)
        greeted = greeted + exists(step).astype(jnp.int32)
    for k in range(1, ny):
        pl.semaphore_signal(barrier, inc=1, device_id=device("gy", lax.rem(gy + k, ny)), device_id_type=MESH)
    greeted = greeted + (ny - 1)

    row = lax.broadcasted_iota(jnp.int32, (XR, ZR), 0)
    lane = lax.broadcasted_iota(jnp.int32, (XR, ZR), 1)
    real = ((row < X) | ((row < X + RIM) & has("gx", 1)) | ((row >= X + RIM) & has("gx", 0))) & (
        (lane < Z) | ((lane < Z + Z // 2) & has("gz", 1)) | ((lane >= Z + Z // 2) & has("gz", 0)))
    mask[...] = jnp.where(real, 1.0, 0.0)

    for fetch in fetches:
        fetch.wait()

    for c in range(3):
        flat[c] = magnet[c].astype(jnp.float32)
    for y in range(Y):
        rows = pl.ds(y, X, stride=Y)
        kind = phase[rows, :]
        magnetic = kind == 0
        mu = jnp.where(magnetic, 4.0, jnp.where(kind == 1, 1.5, 1.0)).astype(jnp.float32) * perm[rows, :]
        diag[y] = 6.0 * mu
        for c in range(3):
            mom[c, RIM + y, 0:X, 0:Z] = jnp.where(magnetic, flat[c, rows, :], 0.0)

    for buffer in (rx_m, rx_s, rx_g):
        for side in (0, 1):
            @pl.when(jnp.logical_not(has("gx", side)))
            def _():
                buffer[side] = jnp.zeros(buffer.shape[1:], jnp.float32)
    for buffer in (rx_m, rx_s, rx_g):
        for side, first in ((0, 0), (1, RIM + Y)):
            @pl.when(jnp.logical_not(has("gy", side)))
            def _():
                for way in (0, 1):
                    for c in range(buffer.shape[1]):
                        buffer[way, c, first:first + RIM] = jnp.zeros((RIM, 2 * RIM, Z), jnp.float32)
    for buffer in (rz_a, rz_m, rz_s, rz_g):
        for side in (0, 1):
            @pl.when(jnp.logical_not(has("gz", side)))
            def _():
                buffer[side] = jnp.zeros(buffer.shape[1:], jnp.float32)
    for buffer in (mom, src, load):
        for side, first in ((0, 0), (1, RIM + Y)):
            @pl.when(jnp.logical_not(has("gy", side)))
            def _():
                for c in range(3 if buffer is not src else 1):
                    buffer[c, first:first + RIM] = jnp.zeros((RIM, XR, ZR), jnp.float32)

    pl.semaphore_wait(barrier, greeted)

    def copy_of(piece, number):
        step, source, target = piece
        return pltpu.make_async_remote_copy(
            src_ref=source, dst_ref=target, send_sem=send_sem.at[number], recv_sem=recv_sem.at[number],
            device_id=beside(step), device_id_type=MESH)

    def begin(pieces, base):
        for number, piece in enumerate(pieces):
            @pl.when(exists(piece[0]))
            def _():
                copy_of(piece, base + number).start()

    def finish(pieces, base):
        for number, piece in enumerate(pieces):
            @pl.when(exists(piece[0]))
            def _():
                copy_of(piece, base + number).wait_send()
            @pl.when(exists([-move for move in piece[0]]))
            def _():
                copy_of(piece, base + number).wait_recv()

    def flat_pieces(buffer, width, rx):
        planes = {-1: slice(RIM, RIM + width), 0: slice(RIM, RIM + Y), 1: slice(RIM + Y - width, RIM + Y)}
        landing = {-1: slice(RIM + Y, RIM + Y + width), 0: slice(RIM, RIM + Y), 1: slice(RIM - width, RIM)}
        rows = {-1: slice(0, 2 * RIM), 1: slice(X - 2 * RIM, X)}
        pieces = []
        for dy in (-1, 1):
            pieces.append(((0, dy, 0), buffer.at[:, planes[dy], 0:X, 0:Z], buffer.at[:, landing[dy], 0:X, 0:Z]))
        for dy in (0, -1, 1):
            for dx in (-1, 1):
                pieces.append(((dx, dy, 0), buffer.at[:, planes[dy], rows[dx], 0:Z],
                               rx.at[1 if dx < 0 else 0, :, landing[dy]]))
        return pieces

    def place_rows(buffer, parts, width, rx):
        upper = lax.broadcasted_iota(jnp.int32, (Y + 2 * width, 2 * RIM, Z), 1) < RIM
        span = slice(RIM - width, RIM + Y + width)
        for c in range(parts):
            buffer[c, span, X:XR, 0:Z] = jnp.where(upper, rx[1, c, span], rx[0, c, span])

    block = lax.rem(lax.broadcasted_iota(jnp.int32, (XR, Z), 1) + RIM, Z) // (2 * RIM)
    from_after = lax.rem(lax.broadcasted_iota(jnp.int32, (XR, Z), 1), 2 * RIM) < RIM

    def pack(buffer, components, width, rows, tz):
        for at, c in enumerate(components):
            packed = jnp.zeros((rows, Z), jnp.float32)
            for y in range(RIM - width, RIM + Y + width):
                packed = jnp.where(
                    block[0:rows] == y, pltpu.roll(buffer[c, y, 0:rows, 0:Z], (2 * RIM * y) % Z, 1), packed)
            tz[at] = packed

    def unpack(buffer, components, width, rows, rz):
        for at, c in enumerate(components):
            both = jnp.where(from_after[0:rows], rz[1, at], rz[0, at])
            for y in range(RIM - width, RIM + Y + width):
                buffer[c, y, 0:rows, Z:ZR] = pltpu.roll(both, (-2 * RIM * y) % Z, 1)

    def deep_pieces(tz, rz):
        return [((0, 0, -1), tz, rz.at[1]), ((0, 0, 1), tz, rz.at[0])]

    def clear_outside(buffer, parts):
        for side, first in ((0, 0), (1, RIM + Y)):
            @pl.when(jnp.logical_not(has("gy", side)))
            def _():
                for c in range(parts):
                    buffer[c, first:first + RIM] = jnp.zeros((RIM, XR, ZR), jnp.float32)

    flat_m = flat_pieces(mom, 1, rx_m)
    deep_a = deep_pieces(tz_a, rz_a)
    begin(flat_m, 0)
    pack(mom, (2,), 0, X, tz_a)
    begin(deep_a, 8)
    finish(flat_m, 0)
    place_rows(mom, 3, 1, rx_m)
    finish(deep_a, 8)
    unpack(mom, (2,), 0, X, rz_a)

    @pl.loop(RIM, RIM + Y)
    def _(y):
        xp, xm = sides(mom[0, y], 0)
        zp, zm = sides(mom[2, y], 1)
        total = (xp - xm) + (mom[1, y + 1] - mom[1, y - 1]) + (zp - zm)
        src[0, y, 0:X, 0:Z] = -0.5 * total[0:X, 0:Z] / diag[y - RIM]

    flat_s = flat_pieces(src, 4, rx_s)
    deep_s = deep_pieces(tz_s, rz_s)
    deep_m = deep_pieces(tz_m, rz_m)
    begin(flat_s, 10)
    pack(mom, (0, 1, 2), 1, XR, tz_m)
    begin(deep_m, 18)
    finish(flat_s, 10)
    place_rows(src, 1, 4, rx_s)
    pack(src, (0,), 4, XR, tz_s)
    begin(deep_s, 20)

    span = X // ny
    for k in range(1, ny):
        peer = lax.rem(gy + k, ny)
        pltpu.make_async_remote_copy(
            src_ref=stiff.at[:, pl.ds(pl.multiple_of(peer * Y, Y), Y), :],
            dst_ref=modulus.at[pl.ds(gy * span, span)],
            send_sem=g_send.at[k], recv_sem=g_recv.at[k],
            device_id=device("gy", peer), device_id_type=MESH).start()
    own = pltpu.make_async_copy(
        stiff.at[:, pl.ds(pl.multiple_of(gy * Y, Y), Y), :], modulus.at[pl.ds(gy * span, span)], g_local)
    own.start()

    finish(deep_s, 20)
    unpack(src, (0,), 4, XR, rz_s)
    w = chebyshev_weights(1.0, 0.9, SWEEPS)

    def neighbours(buffer, y):
        xp, xm = sides(buffer[0, y], 0)
        zp, zm = sides(buffer[0, y], 1)
        return xp + xm + buffer[0, y + 1] + buffer[0, y - 1] + zp + zm

    @pl.loop(1, 2 * RIM + Y - 1)
    def _(y):
        pot1[0, y] = mask[...] * ((w[0] + w[1] - w[0] * w[1]) * src[0, y] + (w[0] * w[1] / 6.0) * neighbours(src, y))

    clear_outside(pot1, 1)

    @pl.loop(2, 2 * RIM + Y - 2)
    def _(y):
        center = pot1[0, y]
        pot2[0, y] = mask[...] * (center + w[2] * (src[0, y] - center + neighbours(pot1, y) * (1.0 / 6.0)))

    clear_outside(pot2, 1)

    finish(deep_m, 18)
    unpack(mom, (0, 1, 2), 1, XR, rz_m)

    @pl.loop(RIM - 1, RIM + Y + 1)
    def _(y):
        center = pot2[0, y]
        xp, xm = sides(center, 0)
        zp, zm = sides(center, 1)
        m = [mom[c, y] for c in range(3)]
        grad = [xp - xm, pot2[0, y + 1] - pot2[0, y - 1], zp - zm]
        total = [m[c] - 0.5 * grad[c] for c in range(3)]
        inner = (m[0] * total[0] + m[1] * total[1] + m[2] * total[2]) / 3.0
        for number, (a, b) in enumerate(STRAIN_PAIRS):
            if a == b:
                value = MAGNETO * (m[a] * total[a] - inner)
            else:
                value = (0.5 * MAGNETO) * (m[a] * total[b] + m[b] * total[a])
            stress[number, y] = value

    for k in range(1, ny):
        peer = lax.rem(gy + k, ny)
        copy = pltpu.make_async_remote_copy(
            src_ref=stiff.at[:, pl.ds(pl.multiple_of(peer * Y, Y), Y), :],
            dst_ref=modulus.at[pl.ds(lax.rem(gy + ny - k, ny) * span, span)],
            send_sem=g_send.at[k], recv_sem=g_recv.at[k],
            device_id=device("gy", peer), device_id_type=MESH)
        copy.wait_send()
        copy.wait_recv()
    own.wait()
    for y in range(Y):
        diag[y] = 8.0 * modulus.reshape(X * Y, Z)[pl.ds(y, X, stride=Y), :]

    @pl.loop(RIM, RIM + Y)
    def _(y):
        for a in range(3):
            xp, xm = sides(stress[STRESS_AT[a, 0], y], 0)
            zp, zm = sides(stress[STRESS_AT[a, 2], y], 1)
            n = STRESS_AT[a, 1]
            force = 0.5 * ((xp - xm) + (stress[n, y + 1] - stress[n, y - 1]) + (zp - zm))[0:X, 0:Z]
            load[a, y, 0:X, 0:Z] = force.astype(jnp.bfloat16).astype(jnp.float32) / diag[y - RIM]

    flat_g = flat_pieces(load, 3, rx_g)
    deep_g = deep_pieces(tz_g, rz_g)
    begin(flat_g, 22)
    finish(flat_g, 22)
    place_rows(load, 3, 3, rx_g)
    pack(load, (0, 1, 2), 3, XR, tz_g)
    begin(deep_g, 30)
    finish(deep_g, 30)
    unpack(load, (0, 1, 2), 3, XR, rz_g)
    v = chebyshev_weights(1.3, 1.2, SWEEPS)

    def navier(buffer, y):
        u = [buffer[c, y] for c in range(3)]
        up = [buffer[c, y + 1] for c in range(3)]
        um = [buffer[c, y - 1] for c in range(3)]
        xs = [sides(u[c], 0) for c in range(3)]
        zs = [sides(u[c], 1) for c in range(3)]
        dy = [up[c] - um[c] for c in range(3)]
        dx0 = xs[0][0] - xs[0][1]
        dz2 = zs[2][0] - zs[2][1]
        ap, am = sides(dy[1] + dz2, 0)
        bp, bm = sides(dy[0], 0)
        cp, cm = sides(dy[2], 1)
        ep, em = sides(dx0 + dy[1], 1)
        mixed = [ap - am, (bp - bm) + (cp - cm), ep - em]
        result = []
        for c in range(3):
            along = [xs[c][0] + xs[c][1], up[c] + um[c], zs[c][0] + zs[c][1]]
            rest = along[0] + along[1] + along[2] + along[c]
            result.append(8.0 * u[c] - rest - 0.25 * mixed[c])
        return u, result

    @pl.loop(2, 2 * RIM + Y - 2)
    def _(y):
        u, result = navier(load, y)
        for c in range(3):
            disp1[c, y] = mask[...] * ((v[0] + v[1]) * u[c] - (v[0] * v[1] / 8.0) * result[c])

    clear_outside(disp1, 3)

    @pl.loop(3, 2 * RIM + Y - 3)
    def _(y):
        u, result = navier(disp1, y)
        for c in range(3):
            disp2[c, y] = mask[...] * (u[c] + v[2] * (load[c, y] - 0.125 * result[c]))

    clear_outside(disp2, 3)

    for y in range(RIM, RIM + Y):
        rows = pl.ds(y - RIM, X, stride=Y)
        gradient = {}
        for c in range(3):
            u = disp2[c, y]
            xp, xm = sides(u, 0)
            zp, zm = sides(u, 1)
            gradient[c, 0] = (xp - xm)[0:X, 0:Z]
            gradient[c, 1] = (disp2[c, y + 1] - disp2[c, y - 1])[0:X, 0:Z]
            gradient[c, 2] = (zp - zm)[0:X, 0:Z]
        for number, (a, b) in enumerate(STRAIN_PAIRS):
            flat[number, rows, :] = 0.25 * (gradient[b, a] + gradient[a, b])
    for number in range(6):
        out[number] = flat[number].astype(jnp.bfloat16)


def per_device(phase, perm_scale, magnetization, stiffness):
    X, Y, Z = phase.shape
    nx, ny, nz = (lax.axis_size(axis) for axis in ("gx", "gy", "gz"))
    XR, ZR, P2 = X + 2 * RIM, 2 * Z, Y + 2 * RIM
    f32 = jnp.float32
    field = lambda parts: pltpu.VMEM((parts, P2, XR, ZR), f32)
    rx = lambda parts: pltpu.VMEM((2, parts, P2, 2 * RIM, Z), f32)
    vmem = pl.BlockSpec(memory_space=pltpu.VMEM)
    result = pl.pallas_call(
        functools.partial(kernel, (nx, ny, nz, X, Y, Z)),
        out_shape=jax.ShapeDtypeStruct((6, X * Y, Z), jnp.bfloat16),
        in_specs=[pl.BlockSpec(memory_space=pl.ANY)] * 4,
        out_specs=vmem,
        scratch_shapes=[
            pltpu.VMEM((X * Y, Z), jnp.int32), pltpu.VMEM((X * Y, Z), f32), pltpu.VMEM((3, X * Y, Z), jnp.bfloat16),
            pltpu.SemaphoreType.DMA((3,)),
            pltpu.VMEM((6, X * Y, Z), f32), pltpu.VMEM((Y, X, Z), f32),
            field(3), field(1), field(1), field(1), field(6), field(3), field(3), field(3),
            pltpu.VMEM((XR, ZR), f32), pltpu.VMEM((X, Y, Z), f32),
            rx(3), rx(1), rx(3),
            pltpu.VMEM((1, X, Z), f32), pltpu.VMEM((3, XR, Z), f32), pltpu.VMEM((1, XR, Z), f32), pltpu.VMEM((3, XR, Z), f32),
            pltpu.VMEM((2, 1, X, Z), f32), pltpu.VMEM((2, 3, XR, Z), f32), pltpu.VMEM((2, 1, XR, Z), f32), pltpu.VMEM((2, 3, XR, Z), f32),
            pltpu.SemaphoreType.DMA((32,)), pltpu.SemaphoreType.DMA((32,)),
            pltpu.SemaphoreType.DMA((ny,)), pltpu.SemaphoreType.DMA((ny,)), pltpu.SemaphoreType.DMA,
        ],
        compiler_params=pltpu.CompilerParams(
            collective_id=0, has_side_effects=True, vmem_limit_bytes=60 * 1024 * 1024),
    )(phase.reshape(X * Y, Z), perm_scale.reshape(X * Y, Z), magnetization.reshape(3, X * Y, Z), stiffness)
    return result.reshape(6, X, Y, Z)


def solution(mesh):
    placed = (
        P("gx", "gy", "gz"),
        P("gx", "gy", "gz"),
        P(None, "gx", "gy", "gz"),
        P(("gx", "gy"), None, "gz"),
    )
    return jax.shard_map(
        per_device, mesh=mesh, in_specs=placed, out_specs=P(None, "gx", "gy", "gz"), check_vma=False
    )
```

```python
import functools
import math

import jax
import jax.numpy as jnp
from jax import lax
from jax.experimental import pallas as pl
from jax.experimental.pallas import tpu as pltpu
from jax.sharding import PartitionSpec as P

SWEEPS = 3
STRAIN_PAIRS = ((0, 0), (1, 1), (2, 2), (0, 1), (1, 2), (0, 2))
STRESS_AT = {(0, 0): 0, (1, 1): 1, (2, 2): 2, (0, 1): 3, (1, 0): 3, (1, 2): 4, (2, 1): 4, (0, 2): 5, (2, 0): 5}
MAGNETO = 4.0
MESH = pl.DeviceIdType.MESH
RIM = 4


def chebyshev_weights(middle, radius, count):
    return [
        1.0 / (middle + radius * math.cos((2 * counter + 1) * math.pi / (2 * count)))
        for counter in range(count)
    ]


def shift(value, dimension, step):
    size = value.shape[dimension]
    return pltpu.roll(value, (-step) % size, dimension)


def sides(value, dimension):
    return shift(value, dimension, 1), shift(value, dimension, -1)


def kernel(sizes, phase_in, perm_in, magnet_in, stiff, out, phase, perm, magnet, in_sem, flat, diag, mom, src, pot1, pot2, stress, load, disp1, disp2,
           mask, modulus, rx_m, rx_s, rx_g, tz_a, tz_m, tz_s, tz_g, rz_a, rz_m, rz_s, rz_g, send_sem, recv_sem, g_send, g_recv, g_local):
    nx, ny, nz, X, Y, Z = sizes
    XR, ZR = X + 2 * RIM, 2 * Z
    gx, gy, gz = lax.axis_index("gx"), lax.axis_index("gy"), lax.axis_index("gz")
    place = {"gx": gx, "gy": gy, "gz": gz}
    count = {"gx": nx, "gy": ny, "gz": nz}

    fetches = [pltpu.make_async_copy(a, b, in_sem.at[i]) for i, (a, b) in enumerate(
        ((magnet_in, magnet), (phase_in, phase), (perm_in, perm)))]
    for fetch in fetches:
        fetch.start()

    def has(axis, side):
        return place[axis] > 0 if side == 0 else place[axis] < count[axis] - 1

    def device(axis, index):
        at = dict(place)
        at[axis] = index
        return (at["gx"], at["gy"], at["gz"])

    def exists(step):
        there = None
        for axis, move in zip(("gx", "gy", "gz"), step):
            if move:
                this = has(axis, 0 if move < 0 else 1)
                there = this if there is None else there & this
        return there

    def beside(step):
        return (gx + step[0], gy + step[1], gz + step[2])

    barrier = pltpu.get_barrier_semaphore()
    greeted = 0
    diagonals = [(dx, dy, 0) for dx in (-1, 1) for dy in (-1, 1)]
    for step in [(-1, 0, 0), (1, 0, 0), (0, 0, -1), (0, 0, 1)] + diagonals:
        @pl.when(exists(step))
        def _():
            pl.semaphore_signal(barrier, inc=1, device_id=beside(step), device_id_type=MESH)
        greeted = greeted + exists(step).astype(jnp.int32)
    for k in range(1, ny):
        pl.semaphore_signal(barrier, inc=1, device_id=device("gy", lax.rem(gy + k, ny)), device_id_type=MESH)
    greeted = greeted + (ny - 1)

    row = lax.broadcasted_iota(jnp.int32, (XR, ZR), 0)
    lane = lax.broadcasted_iota(jnp.int32, (XR, ZR), 1)
    real = ((row < X) | ((row < X + RIM) & has("gx", 1)) | ((row >= X + RIM) & has("gx", 0))) & (
        (lane < Z) | ((lane < Z + Z // 2) & has("gz", 1)) | ((lane >= Z + Z // 2) & has("gz", 0)))
    mask[...] = jnp.where(real, 1.0, 0.0)

    for fetch in fetches:
        fetch.wait()

    for c in range(3):
        flat[c] = magnet[c].astype(jnp.float32)
    for y in range(Y):
        rows = pl.ds(y, X, stride=Y)
        kind = phase[rows, :]
        magnetic = kind == 0
        mu = jnp.where(magnetic, 4.0, jnp.where(kind == 1, 1.5, 1.0)).astype(jnp.float32) * perm[rows, :]
        diag[y] = 6.0 * mu
        for c in range(3):
            mom[c, RIM + y, 0:X, 0:Z] = jnp.where(magnetic, flat[c, rows, :], 0.0)

    for buffer in (rx_m, rx_s, rx_g):
        for side in (0, 1):
            @pl.when(jnp.logical_not(has("gx", side)))
            def _():
                buffer[side] = jnp.zeros(buffer.shape[1:], jnp.float32)
    for buffer in (rx_m, rx_s, rx_g):
        for side, first in ((0, 0), (1, RIM + Y)):
            @pl.when(jnp.logical_not(has("gy", side)))
            def _():
                for way in (0, 1):
                    for c in range(buffer.shape[1]):
                        buffer[way, c, first:first + RIM] = jnp.zeros((RIM, 2 * RIM, Z), jnp.float32)
    for buffer in (rz_a, rz_m, rz_s, rz_g):
        for side in (0, 1):
            @pl.when(jnp.logical_not(has("gz", side)))
            def _():
                buffer[side] = jnp.zeros(buffer.shape[1:], jnp.float32)
    for buffer in (mom, src, load):
        for side, first in ((0, 0), (1, RIM + Y)):
            @pl.when(jnp.logical_not(has("gy", side)))
            def _():
                for c in range(3 if buffer is not src else 1):
                    buffer[c, first:first + RIM] = jnp.zeros((RIM, XR, ZR), jnp.float32)

    pl.semaphore_wait(barrier, greeted)

    def copy_of(piece, number):
        step, source, target = piece
        return pltpu.make_async_remote_copy(
            src_ref=source, dst_ref=target, send_sem=send_sem.at[number], recv_sem=recv_sem.at[number],
            device_id=beside(step), device_id_type=MESH)

    def begin(pieces, base):
        for number, piece in enumerate(pieces):
            @pl.when(exists(piece[0]))
            def _():
                copy_of(piece, base + number).start()

    def finish(pieces, base):
        for number, piece in enumerate(pieces):
            @pl.when(exists(piece[0]))
            def _():
                copy_of(piece, base + number).wait_send()
            @pl.when(exists([-move for move in piece[0]]))
            def _():
                copy_of(piece, base + number).wait_recv()

    def flat_pieces(buffer, width, rx, parts=slice(None)):
        planes = {-1: slice(RIM, RIM + width), 0: slice(RIM, RIM + Y), 1: slice(RIM + Y - width, RIM + Y)}
        landing = {-1: slice(RIM + Y, RIM + Y + width), 0: slice(RIM, RIM + Y), 1: slice(RIM - width, RIM)}
        rows = {-1: slice(0, 2 * RIM), 1: slice(X - 2 * RIM, X)}
        pieces = []
        for dy in (-1, 1):
            pieces.append(((0, dy, 0), buffer.at[parts, planes[dy], 0:X, 0:Z], buffer.at[parts, landing[dy], 0:X, 0:Z]))
        for dy in (0, -1, 1):
            for dx in (-1, 1):
                pieces.append(((dx, dy, 0), buffer.at[parts, planes[dy], rows[dx], 0:Z],
                               rx.at[1 if dx < 0 else 0, parts, landing[dy]]))
        return pieces

    def place_rows(buffer, components, width, rx):
        upper = lax.broadcasted_iota(jnp.int32, (Y + 2 * width, 2 * RIM, Z), 1) < RIM
        span = slice(RIM - width, RIM + Y + width)
        for c in components:
            buffer[c, span, X:XR, 0:Z] = jnp.where(upper, rx[1, c, span], rx[0, c, span])

    block = lax.rem(lax.broadcasted_iota(jnp.int32, (XR, Z), 1) + RIM, Z) // (2 * RIM)
    from_after = lax.rem(lax.broadcasted_iota(jnp.int32, (XR, Z), 1), 2 * RIM) < RIM

    def pack(buffer, components, width, rows, tz, first=0):
        for at, c in enumerate(components, first):
            packed = jnp.zeros((rows, Z), jnp.float32)
            for y in range(RIM - width, RIM + Y + width):
                packed = jnp.where(
                    block[0:rows] == y, pltpu.roll(buffer[c, y, 0:rows, 0:Z], (2 * RIM * y) % Z, 1), packed)
            tz[at] = packed

    def unpack(buffer, components, width, rows, rz, first=0):
        for at, c in enumerate(components, first):
            both = jnp.where(from_after[0:rows], rz[1, at], rz[0, at])
            for y in range(RIM - width, RIM + Y + width):
                buffer[c, y, 0:rows, Z:ZR] = pltpu.roll(both, (-2 * RIM * y) % Z, 1)

    def deep_pieces(tz, rz, parts=slice(None)):
        return [((0, 0, -1), tz.at[parts], rz.at[1, parts]), ((0, 0, 1), tz.at[parts], rz.at[0, parts])]

    def clear_outside(buffer, parts):
        for side, first in ((0, 0), (1, RIM + Y)):
            @pl.when(jnp.logical_not(has("gy", side)))
            def _():
                for c in range(parts):
                    buffer[c, first:first + RIM] = jnp.zeros((RIM, XR, ZR), jnp.float32)

    flat_m = flat_pieces(mom, 1, rx_m)
    deep_a = deep_pieces(tz_a, rz_a)
    begin(flat_m, 0)
    pack(mom, (2,), 0, X, tz_a)
    begin(deep_a, 8)
    finish(flat_m, 0)
    place_rows(mom, (0, 1, 2), 1, rx_m)
    finish(deep_a, 8)
    unpack(mom, (2,), 0, X, rz_a)

    @pl.loop(RIM, RIM + Y)
    def _(y):
        xp, xm = sides(mom[0, y], 0)
        zp, zm = sides(mom[2, y], 1)
        total = (xp - xm) + (mom[1, y + 1] - mom[1, y - 1]) + (zp - zm)
        src[0, y, 0:X, 0:Z] = -0.5 * total[0:X, 0:Z] / diag[y - RIM]

    flat_s = flat_pieces(src, 4, rx_s)
    deep_s = deep_pieces(tz_s, rz_s)
    deep_m = deep_pieces(tz_m, rz_m)
    begin(flat_s, 10)
    pack(mom, (0, 1, 2), 1, XR, tz_m)
    begin(deep_m, 18)
    finish(flat_s, 10)
    place_rows(src, (0,), 4, rx_s)
    pack(src, (0,), 4, XR, tz_s)
    begin(deep_s, 20)

    span = X // ny
    for k in range(1, ny):
        peer = lax.rem(gy + k, ny)
        pltpu.make_async_remote_copy(
            src_ref=stiff.at[:, pl.ds(pl.multiple_of(peer * Y, Y), Y), :],
            dst_ref=modulus.at[pl.ds(gy * span, span)],
            send_sem=g_send.at[k], recv_sem=g_recv.at[k],
            device_id=device("gy", peer), device_id_type=MESH).start()
    own = pltpu.make_async_copy(
        stiff.at[:, pl.ds(pl.multiple_of(gy * Y, Y), Y), :], modulus.at[pl.ds(gy * span, span)], g_local)
    own.start()

    finish(deep_s, 20)
    unpack(src, (0,), 4, XR, rz_s)
    w = chebyshev_weights(1.0, 0.9, SWEEPS)

    def neighbours(buffer, y):
        xp, xm = sides(buffer[0, y], 0)
        zp, zm = sides(buffer[0, y], 1)
        return xp + xm + buffer[0, y + 1] + buffer[0, y - 1] + zp + zm

    @pl.loop(1, 2 * RIM + Y - 1)
    def _(y):
        pot1[0, y] = mask[...] * ((w[0] + w[1] - w[0] * w[1]) * src[0, y] + (w[0] * w[1] / 6.0) * neighbours(src, y))

    clear_outside(pot1, 1)

    @pl.loop(2, 2 * RIM + Y - 2)
    def _(y):
        center = pot1[0, y]
        pot2[0, y] = mask[...] * (center + w[2] * (src[0, y] - center + neighbours(pot1, y) * (1.0 / 6.0)))

    clear_outside(pot2, 1)

    finish(deep_m, 18)
    unpack(mom, (0, 1, 2), 1, XR, rz_m)

    @pl.loop(RIM - 1, RIM + Y + 1)
    def _(y):
        center = pot2[0, y]
        xp, xm = sides(center, 0)
        zp, zm = sides(center, 1)
        m = [mom[c, y] for c in range(3)]
        grad = [xp - xm, pot2[0, y + 1] - pot2[0, y - 1], zp - zm]
        total = [m[c] - 0.5 * grad[c] for c in range(3)]
        inner = (m[0] * total[0] + m[1] * total[1] + m[2] * total[2]) / 3.0
        for number, (a, b) in enumerate(STRAIN_PAIRS):
            if a == b:
                value = MAGNETO * (m[a] * total[a] - inner)
            else:
                value = (0.5 * MAGNETO) * (m[a] * total[b] + m[b] * total[a])
            stress[number, y] = value

    for k in range(1, ny):
        peer = lax.rem(gy + k, ny)
        copy = pltpu.make_async_remote_copy(
            src_ref=stiff.at[:, pl.ds(pl.multiple_of(peer * Y, Y), Y), :],
            dst_ref=modulus.at[pl.ds(lax.rem(gy + ny - k, ny) * span, span)],
            send_sem=g_send.at[k], recv_sem=g_recv.at[k],
            device_id=device("gy", peer), device_id_type=MESH)
        copy.wait_send()
        copy.wait_recv()
    own.wait()
    for y in range(Y):
        diag[y] = 8.0 * modulus.reshape(X * Y, Z)[pl.ds(y, X, stride=Y), :]

    flat_g = [flat_pieces(load, 3, rx_g, slice(a, a + 1)) for a in range(3)]
    deep_g = [deep_pieces(tz_g, rz_g, slice(a, a + 1)) for a in range(3)]
    for a in range(3):
        @pl.loop(RIM, RIM + Y)
        def _(y):
            xp, xm = sides(stress[STRESS_AT[a, 0], y], 0)
            zp, zm = sides(stress[STRESS_AT[a, 2], y], 1)
            n = STRESS_AT[a, 1]
            force = 0.5 * ((xp - xm) + (stress[n, y + 1] - stress[n, y - 1]) + (zp - zm))[0:X, 0:Z]
            load[a, y, 0:X, 0:Z] = force.astype(jnp.bfloat16).astype(jnp.float32) / diag[y - RIM]

        begin(flat_g[a], 22 + 10 * a)
    for a in range(3):
        finish(flat_g[a], 22 + 10 * a)
        place_rows(load, (a,), 3, rx_g)
        pack(load, (a,), 3, XR, tz_g, a)
        begin(deep_g[a], 30 + 10 * a)
    for a in range(3):
        finish(deep_g[a], 30 + 10 * a)
        unpack(load, (a,), 3, XR, rz_g, a)
    v = chebyshev_weights(1.3, 1.2, SWEEPS)

    def navier(buffer, y):
        u = [buffer[c, y] for c in range(3)]
        up = [buffer[c, y + 1] for c in range(3)]
        um = [buffer[c, y - 1] for c in range(3)]
        xs = [sides(u[c], 0) for c in range(3)]
        zs = [sides(u[c], 1) for c in range(3)]
        dy = [up[c] - um[c] for c in range(3)]
        dx0 = xs[0][0] - xs[0][1]
        dz2 = zs[2][0] - zs[2][1]
        ap, am = sides(dy[1] + dz2, 0)
        bp, bm = sides(dy[0], 0)
        cp, cm = sides(dy[2], 1)
        ep, em = sides(dx0 + dy[1], 1)
        mixed = [ap - am, (bp - bm) + (cp - cm), ep - em]
        result = []
        for c in range(3):
            along = [xs[c][0] + xs[c][1], up[c] + um[c], zs[c][0] + zs[c][1]]
            rest = along[0] + along[1] + along[2] + along[c]
            result.append(8.0 * u[c] - rest - 0.25 * mixed[c])
        return u, result

    @pl.loop(2, 2 * RIM + Y - 2)
    def _(y):
        u, result = navier(load, y)
        for c in range(3):
            disp1[c, y] = mask[...] * ((v[0] + v[1]) * u[c] - (v[0] * v[1] / 8.0) * result[c])

    clear_outside(disp1, 3)

    @pl.loop(3, 2 * RIM + Y - 3)
    def _(y):
        u, result = navier(disp1, y)
        for c in range(3):
            disp2[c, y] = mask[...] * (u[c] + v[2] * (load[c, y] - 0.125 * result[c]))

    clear_outside(disp2, 3)

    for y in range(RIM, RIM + Y):
        rows = pl.ds(y - RIM, X, stride=Y)
        gradient = {}
        for c in range(3):
            u = disp2[c, y]
            xp, xm = sides(u, 0)
            zp, zm = sides(u, 1)
            gradient[c, 0] = (xp - xm)[0:X, 0:Z]
            gradient[c, 1] = (disp2[c, y + 1] - disp2[c, y - 1])[0:X, 0:Z]
            gradient[c, 2] = (zp - zm)[0:X, 0:Z]
        for number, (a, b) in enumerate(STRAIN_PAIRS):
            flat[number, rows, :] = 0.25 * (gradient[b, a] + gradient[a, b])
    for number in range(6):
        out[number] = flat[number].astype(jnp.bfloat16)


def per_device(phase, perm_scale, magnetization, stiffness):
    X, Y, Z = phase.shape
    nx, ny, nz = (lax.axis_size(axis) for axis in ("gx", "gy", "gz"))
    XR, ZR, P2 = X + 2 * RIM, 2 * Z, Y + 2 * RIM
    f32 = jnp.float32
    field = lambda parts: pltpu.VMEM((parts, P2, XR, ZR), f32)
    rx = lambda parts: pltpu.VMEM((2, parts, P2, 2 * RIM, Z), f32)
    vmem = pl.BlockSpec(memory_space=pltpu.VMEM)
    result = pl.pallas_call(
        functools.partial(kernel, (nx, ny, nz, X, Y, Z)),
        out_shape=jax.ShapeDtypeStruct((6, X * Y, Z), jnp.bfloat16),
        in_specs=[pl.BlockSpec(memory_space=pl.ANY)] * 4,
        out_specs=vmem,
        scratch_shapes=[
            pltpu.VMEM((X * Y, Z), jnp.int32), pltpu.VMEM((X * Y, Z), f32), pltpu.VMEM((3, X * Y, Z), jnp.bfloat16),
            pltpu.SemaphoreType.DMA((3,)),
            pltpu.VMEM((6, X * Y, Z), f32), pltpu.VMEM((Y, X, Z), f32),
            field(3), field(1), field(1), field(1), field(6), field(3), field(3), field(3),
            pltpu.VMEM((XR, ZR), f32), pltpu.VMEM((X, Y, Z), f32),
            rx(3), rx(1), rx(3),
            pltpu.VMEM((1, X, Z), f32), pltpu.VMEM((3, XR, Z), f32), pltpu.VMEM((1, XR, Z), f32), pltpu.VMEM((3, XR, Z), f32),
            pltpu.VMEM((2, 1, X, Z), f32), pltpu.VMEM((2, 3, XR, Z), f32), pltpu.VMEM((2, 1, XR, Z), f32), pltpu.VMEM((2, 3, XR, Z), f32),
            pltpu.SemaphoreType.DMA((52,)), pltpu.SemaphoreType.DMA((52,)),
            pltpu.SemaphoreType.DMA((ny,)), pltpu.SemaphoreType.DMA((ny,)), pltpu.SemaphoreType.DMA,
        ],
        compiler_params=pltpu.CompilerParams(
            collective_id=0, has_side_effects=True, vmem_limit_bytes=60 * 1024 * 1024),
    )(phase.reshape(X * Y, Z), perm_scale.reshape(X * Y, Z), magnetization.reshape(3, X * Y, Z), stiffness)
    return result.reshape(6, X, Y, Z)


def solution(mesh):
    placed = (
        P("gx", "gy", "gz"),
        P("gx", "gy", "gz"),
        P(None, "gx", "gy", "gz"),
        P(("gx", "gy"), None, "gz"),
    )
    return jax.shard_map(
        per_device, mesh=mesh, in_specs=placed, out_specs=P(None, "gx", "gy", "gz"), check_vma=False
    )
```

```python
import functools
import math

import jax
import jax.numpy as jnp
from jax import lax
from jax.experimental import pallas as pl
from jax.experimental.pallas import tpu as pltpu
from jax.sharding import PartitionSpec as P

SWEEPS = 3
STRAIN_PAIRS = ((0, 0), (1, 1), (2, 2), (0, 1), (1, 2), (0, 2))
STRESS_AT = {(0, 0): 0, (1, 1): 1, (2, 2): 2, (0, 1): 3, (1, 0): 3, (1, 2): 4, (2, 1): 4, (0, 2): 5, (2, 0): 5}
MAGNETO = 4.0
MESH = pl.DeviceIdType.MESH
RIM = 4


def chebyshev_weights(middle, radius, count):
    return [
        1.0 / (middle + radius * math.cos((2 * counter + 1) * math.pi / (2 * count)))
        for counter in range(count)
    ]


def shift(value, dimension, step):
    size = value.shape[dimension]
    return pltpu.roll(value, (-step) % size, dimension)


def sides(value, dimension):
    return shift(value, dimension, 1), shift(value, dimension, -1)


def kernel(sizes, phase_in, perm_in, magnet_in, stiff, out, phase, perm, magnet, in_sem, flat, diag, mom, src, pot1, pot2, stress, load, disp1, disp2,
           mask, modulus, rx_m, rx_s, rx_g, tz_a, tz_m, tz_s, tz_g, rz_a, rz_m, rz_s, rz_g, send_sem, recv_sem, g_send, g_recv, g_local):
    nx, ny, nz, X, Y, Z = sizes
    XR, ZR = X + 2 * RIM, 2 * Z
    gx, gy, gz = lax.axis_index("gx"), lax.axis_index("gy"), lax.axis_index("gz")
    place = {"gx": gx, "gy": gy, "gz": gz}
    count = {"gx": nx, "gy": ny, "gz": nz}

    fetches = [pltpu.make_async_copy(a, b, in_sem.at[i]) for i, (a, b) in enumerate(
        ((magnet_in, magnet), (phase_in, phase), (perm_in, perm)))]
    for fetch in fetches:
        fetch.start()

    def has(axis, side):
        return place[axis] > 0 if side == 0 else place[axis] < count[axis] - 1

    def device(axis, index):
        at = dict(place)
        at[axis] = index
        return (at["gx"], at["gy"], at["gz"])

    def exists(step):
        there = None
        for axis, move in zip(("gx", "gy", "gz"), step):
            if move:
                this = has(axis, 0 if move < 0 else 1)
                there = this if there is None else there & this
        return there

    def beside(step):
        return (gx + step[0], gy + step[1], gz + step[2])

    barrier = pltpu.get_barrier_semaphore()
    greeted = 0
    diagonals = [(dx, dy, 0) for dx in (-1, 1) for dy in (-1, 1)]
    for step in [(-1, 0, 0), (1, 0, 0), (0, 0, -1), (0, 0, 1)] + diagonals:
        @pl.when(exists(step))
        def _():
            pl.semaphore_signal(barrier, inc=1, device_id=beside(step), device_id_type=MESH)
        greeted = greeted + exists(step).astype(jnp.int32)
    for k in range(1, ny):
        pl.semaphore_signal(barrier, inc=1, device_id=device("gy", lax.rem(gy + k, ny)), device_id_type=MESH)
    greeted = greeted + (ny - 1)

    row = lax.broadcasted_iota(jnp.int32, (XR, ZR), 0)
    lane = lax.broadcasted_iota(jnp.int32, (XR, ZR), 1)
    real = ((row < X) | ((row < X + RIM) & has("gx", 1)) | ((row >= X + RIM) & has("gx", 0))) & (
        (lane < Z) | ((lane < Z + Z // 2) & has("gz", 1)) | ((lane >= Z + Z // 2) & has("gz", 0)))
    mask[...] = jnp.where(real, 1.0, 0.0)

    for fetch in fetches:
        fetch.wait()

    for c in range(3):
        flat[c] = magnet[c].astype(jnp.float32)
    for y in range(Y):
        rows = pl.ds(y, X, stride=Y)
        kind = phase[rows, :]
        magnetic = kind == 0
        mu = jnp.where(magnetic, 4.0, jnp.where(kind == 1, 1.5, 1.0)).astype(jnp.float32) * perm[rows, :]
        diag[y] = 6.0 * mu
        for c in range(3):
            mom[c, RIM + y, 0:X, 0:Z] = jnp.where(magnetic, flat[c, rows, :], 0.0)

    for buffer in (rx_m, rx_s, rx_g):
        for side in (0, 1):
            @pl.when(jnp.logical_not(has("gx", side)))
            def _():
                buffer[side] = jnp.zeros(buffer.shape[1:], jnp.float32)
    for buffer in (rx_m, rx_s, rx_g):
        for side, first in ((0, 0), (1, RIM + Y)):
            @pl.when(jnp.logical_not(has("gy", side)))
            def _():
                for way in (0, 1):
                    for c in range(buffer.shape[1]):
                        buffer[way, c, first:first + RIM] = jnp.zeros((RIM, 2 * RIM, Z), jnp.float32)
    for buffer in (rz_a, rz_m, rz_s, rz_g):
        for side in (0, 1):
            @pl.when(jnp.logical_not(has("gz", side)))
            def _():
                buffer[side] = jnp.zeros(buffer.shape[1:], jnp.float32)
    for buffer in (mom, src, load):
        for side, first in ((0, 0), (1, RIM + Y)):
            @pl.when(jnp.logical_not(has("gy", side)))
            def _():
                for c in range(3 if buffer is not src else 1):
                    buffer[c, first:first + RIM] = jnp.zeros((RIM, XR, ZR), jnp.float32)

    pl.semaphore_wait(barrier, greeted)

    def copy_of(piece, number):
        step, source, target = piece
        return pltpu.make_async_remote_copy(
            src_ref=source, dst_ref=target, send_sem=send_sem.at[number], recv_sem=recv_sem.at[number],
            device_id=beside(step), device_id_type=MESH)

    def begin(pieces, base):
        for number, piece in enumerate(pieces):
            @pl.when(exists(piece[0]))
            def _():
                copy_of(piece, base + number).start()

    def finish(pieces, base):
        for number, piece in enumerate(pieces):
            @pl.when(exists(piece[0]))
            def _():
                copy_of(piece, base + number).wait_send()
            @pl.when(exists([-move for move in piece[0]]))
            def _():
                copy_of(piece, base + number).wait_recv()

    def flat_pieces(buffer, width, rx, parts=slice(None)):
        planes = {-1: slice(RIM, RIM + width), 0: slice(RIM, RIM + Y), 1: slice(RIM + Y - width, RIM + Y)}
        landing = {-1: slice(RIM + Y, RIM + Y + width), 0: slice(RIM, RIM + Y), 1: slice(RIM - width, RIM)}
        rows = {-1: slice(0, 2 * RIM), 1: slice(X - 2 * RIM, X)}
        pieces = []
        for dy in (-1, 1):
            pieces.append(((0, dy, 0), buffer.at[parts, planes[dy], 0:X, 0:Z], buffer.at[parts, landing[dy], 0:X, 0:Z]))
        for dy in (0, -1, 1):
            for dx in (-1, 1):
                pieces.append(((dx, dy, 0), buffer.at[parts, planes[dy], rows[dx], 0:Z],
                               rx.at[1 if dx < 0 else 0, parts, landing[dy]]))
        return pieces

    def place_rows(buffer, components, width, rx):
        upper = lax.broadcasted_iota(jnp.int32, (Y + 2 * width, 2 * RIM, Z), 1) < RIM
        span = slice(RIM - width, RIM + Y + width)
        for c in components:
            buffer[c, span, X:XR, 0:Z] = jnp.where(upper, rx[1, c, span], rx[0, c, span])

    block = lax.rem(lax.broadcasted_iota(jnp.int32, (XR, Z), 1) + RIM, Z) // (2 * RIM)
    from_after = lax.rem(lax.broadcasted_iota(jnp.int32, (XR, Z), 1), 2 * RIM) < RIM

    def pack(buffer, components, width, rows, tz, first=0):
        for at, c in enumerate(components, first):
            packed = jnp.zeros((rows, Z), jnp.float32)
            for y in range(RIM - width, RIM + Y + width):
                packed = jnp.where(
                    block[0:rows] == y, pltpu.roll(buffer[c, y, 0:rows, 0:Z], (2 * RIM * y) % Z, 1), packed)
            tz[at] = packed

    def unpack(buffer, components, width, rows, rz, first=0):
        for at, c in enumerate(components, first):
            both = jnp.where(from_after[0:rows], rz[1, at], rz[0, at])
            for y in range(RIM - width, RIM + Y + width):
                buffer[c, y, 0:rows, Z:ZR] = pltpu.roll(both, (-2 * RIM * y) % Z, 1)

    def deep_pieces(tz, rz, parts=slice(None)):
        return [((0, 0, -1), tz.at[parts], rz.at[1, parts]), ((0, 0, 1), tz.at[parts], rz.at[0, parts])]

    def clear_outside(buffer, parts):
        for side, first in ((0, 0), (1, RIM + Y)):
            @pl.when(jnp.logical_not(has("gy", side)))
            def _():
                for c in range(parts):
                    buffer[c, first:first + RIM] = jnp.zeros((RIM, XR, ZR), jnp.float32)

    flat_m = flat_pieces(mom, 1, rx_m)
    deep_a = deep_pieces(tz_a, rz_a)
    begin(flat_m, 0)
    pack(mom, (2,), 0, X, tz_a)
    begin(deep_a, 8)
    finish(flat_m, 0)
    place_rows(mom, (0, 1, 2), 1, rx_m)
    finish(deep_a, 8)
    unpack(mom, (2,), 0, X, rz_a)

    @pl.loop(RIM, RIM + Y, unroll=2)
    def _(y):
        xp, xm = sides(mom[0, y], 0)
        zp, zm = sides(mom[2, y], 1)
        total = (xp - xm) + (mom[1, y + 1] - mom[1, y - 1]) + (zp - zm)
        src[0, y, 0:X, 0:Z] = -0.5 * total[0:X, 0:Z] / diag[y - RIM]

    flat_s = flat_pieces(src, 4, rx_s)
    deep_s = deep_pieces(tz_s, rz_s)
    deep_m = deep_pieces(tz_m, rz_m)
    begin(flat_s, 10)
    pack(mom, (0, 1, 2), 1, XR, tz_m)
    begin(deep_m, 18)
    finish(flat_s, 10)
    place_rows(src, (0,), 4, rx_s)
    pack(src, (0,), 4, XR, tz_s)
    begin(deep_s, 20)

    span = X // ny
    for k in range(1, ny):
        peer = lax.rem(gy + k, ny)
        pltpu.make_async_remote_copy(
            src_ref=stiff.at[:, pl.ds(pl.multiple_of(peer * Y, Y), Y), :],
            dst_ref=modulus.at[pl.ds(gy * span, span)],
            send_sem=g_send.at[k], recv_sem=g_recv.at[k],
            device_id=device("gy", peer), device_id_type=MESH).start()
    own = pltpu.make_async_copy(
        stiff.at[:, pl.ds(pl.multiple_of(gy * Y, Y), Y), :], modulus.at[pl.ds(gy * span, span)], g_local)
    own.start()

    finish(deep_s, 20)
    unpack(src, (0,), 4, XR, rz_s)
    w = chebyshev_weights(1.0, 0.9, SWEEPS)

    def neighbours(buffer, y):
        xp, xm = sides(buffer[0, y], 0)
        zp, zm = sides(buffer[0, y], 1)
        return xp + xm + buffer[0, y + 1] + buffer[0, y - 1] + zp + zm

    @pl.loop(1, 2 * RIM + Y - 1, unroll=2)
    def _(y):
        pot1[0, y] = mask[...] * ((w[0] + w[1] - w[0] * w[1]) * src[0, y] + (w[0] * w[1] / 6.0) * neighbours(src, y))

    clear_outside(pot1, 1)

    @pl.loop(2, 2 * RIM + Y - 2, unroll=2)
    def _(y):
        center = pot1[0, y]
        pot2[0, y] = mask[...] * (center + w[2] * (src[0, y] - center + neighbours(pot1, y) * (1.0 / 6.0)))

    clear_outside(pot2, 1)

    finish(deep_m, 18)
    unpack(mom, (0, 1, 2), 1, XR, rz_m)

    @pl.loop(RIM - 1, RIM + Y + 1, unroll=2)
    def _(y):
        center = pot2[0, y]
        xp, xm = sides(center, 0)
        zp, zm = sides(center, 1)
        m = [mom[c, y] for c in range(3)]
        grad = [xp - xm, pot2[0, y + 1] - pot2[0, y - 1], zp - zm]
        total = [m[c] - 0.5 * grad[c] for c in range(3)]
        inner = (m[0] * total[0] + m[1] * total[1] + m[2] * total[2]) / 3.0
        for number, (a, b) in enumerate(STRAIN_PAIRS):
            if a == b:
                value = MAGNETO * (m[a] * total[a] - inner)
            else:
                value = (0.5 * MAGNETO) * (m[a] * total[b] + m[b] * total[a])
            stress[number, y] = value

    for k in range(1, ny):
        peer = lax.rem(gy + k, ny)
        copy = pltpu.make_async_remote_copy(
            src_ref=stiff.at[:, pl.ds(pl.multiple_of(peer * Y, Y), Y), :],
            dst_ref=modulus.at[pl.ds(lax.rem(gy + ny - k, ny) * span, span)],
            send_sem=g_send.at[k], recv_sem=g_recv.at[k],
            device_id=device("gy", peer), device_id_type=MESH)
        copy.wait_send()
        copy.wait_recv()
    own.wait()
    for y in range(Y):
        diag[y] = 8.0 * modulus.reshape(X * Y, Z)[pl.ds(y, X, stride=Y), :]

    flat_g = [flat_pieces(load, 3, rx_g, slice(a, a + 1)) for a in range(3)]
    deep_g = [deep_pieces(tz_g, rz_g, slice(a, a + 1)) for a in range(3)]
    for a in range(3):
        @pl.loop(RIM, RIM + Y, unroll=2)
        def _(y):
            xp, xm = sides(stress[STRESS_AT[a, 0], y], 0)
            zp, zm = sides(stress[STRESS_AT[a, 2], y], 1)
            n = STRESS_AT[a, 1]
            force = 0.5 * ((xp - xm) + (stress[n, y + 1] - stress[n, y - 1]) + (zp - zm))[0:X, 0:Z]
            load[a, y, 0:X, 0:Z] = force.astype(jnp.bfloat16).astype(jnp.float32) / diag[y - RIM]

        begin(flat_g[a], 22 + 10 * a)
    for a in range(3):
        finish(flat_g[a], 22 + 10 * a)
        place_rows(load, (a,), 3, rx_g)
        pack(load, (a,), 3, XR, tz_g, a)
        begin(deep_g[a], 30 + 10 * a)
    for a in range(3):
        finish(deep_g[a], 30 + 10 * a)
        unpack(load, (a,), 3, XR, rz_g, a)
    v = chebyshev_weights(1.3, 1.2, SWEEPS)

    def navier(buffer, y):
        u = [buffer[c, y] for c in range(3)]
        up = [buffer[c, y + 1] for c in range(3)]
        um = [buffer[c, y - 1] for c in range(3)]
        xs = [sides(u[c], 0) for c in range(3)]
        zs = [sides(u[c], 1) for c in range(3)]
        dy = [up[c] - um[c] for c in range(3)]
        dx0 = xs[0][0] - xs[0][1]
        dz2 = zs[2][0] - zs[2][1]
        ap, am = sides(dy[1] + dz2, 0)
        bp, bm = sides(dy[0], 0)
        cp, cm = sides(dy[2], 1)
        ep, em = sides(dx0 + dy[1], 1)
        mixed = [ap - am, (bp - bm) + (cp - cm), ep - em]
        result = []
        for c in range(3):
            along = [xs[c][0] + xs[c][1], up[c] + um[c], zs[c][0] + zs[c][1]]
            rest = along[0] + along[1] + along[2] + along[c]
            result.append(8.0 * u[c] - rest - 0.25 * mixed[c])
        return u, result

    @pl.loop(2, 2 * RIM + Y - 2, unroll=2)
    def _(y):
        u, result = navier(load, y)
        for c in range(3):
            disp1[c, y] = mask[...] * ((v[0] + v[1]) * u[c] - (v[0] * v[1] / 8.0) * result[c])

    clear_outside(disp1, 3)

    @pl.loop(3, 2 * RIM + Y - 3, unroll=2)
    def _(y):
        u, result = navier(disp1, y)
        for c in range(3):
            disp2[c, y] = mask[...] * (u[c] + v[2] * (load[c, y] - 0.125 * result[c]))

    clear_outside(disp2, 3)

    for y in range(RIM, RIM + Y):
        rows = pl.ds(y - RIM, X, stride=Y)
        gradient = {}
        for c in range(3):
            u = disp2[c, y]
            xp, xm = sides(u, 0)
            zp, zm = sides(u, 1)
            gradient[c, 0] = (xp - xm)[0:X, 0:Z]
            gradient[c, 1] = (disp2[c, y + 1] - disp2[c, y - 1])[0:X, 0:Z]
            gradient[c, 2] = (zp - zm)[0:X, 0:Z]
        for number, (a, b) in enumerate(STRAIN_PAIRS):
            flat[number, rows, :] = 0.25 * (gradient[b, a] + gradient[a, b])
    for number in range(6):
        out[number] = flat[number].astype(jnp.bfloat16)


def per_device(phase, perm_scale, magnetization, stiffness):
    X, Y, Z = phase.shape
    nx, ny, nz = (lax.axis_size(axis) for axis in ("gx", "gy", "gz"))
    XR, ZR, P2 = X + 2 * RIM, 2 * Z, Y + 2 * RIM
    f32 = jnp.float32
    field = lambda parts: pltpu.VMEM((parts, P2, XR, ZR), f32)
    rx = lambda parts: pltpu.VMEM((2, parts, P2, 2 * RIM, Z), f32)
    vmem = pl.BlockSpec(memory_space=pltpu.VMEM)
    result = pl.pallas_call(
        functools.partial(kernel, (nx, ny, nz, X, Y, Z)),
        out_shape=jax.ShapeDtypeStruct((6, X * Y, Z), jnp.bfloat16),
        in_specs=[pl.BlockSpec(memory_space=pl.ANY)] * 4,
        out_specs=vmem,
        scratch_shapes=[
            pltpu.VMEM((X * Y, Z), jnp.int32), pltpu.VMEM((X * Y, Z), f32), pltpu.VMEM((3, X * Y, Z), jnp.bfloat16),
            pltpu.SemaphoreType.DMA((3,)),
            pltpu.VMEM((6, X * Y, Z), f32), pltpu.VMEM((Y, X, Z), f32),
            field(3), field(1), field(1), field(1), field(6), field(3), field(3), field(3),
            pltpu.VMEM((XR, ZR), f32), pltpu.VMEM((X, Y, Z), f32),
            rx(3), rx(1), rx(3),
            pltpu.VMEM((1, X, Z), f32), pltpu.VMEM((3, XR, Z), f32), pltpu.VMEM((1, XR, Z), f32), pltpu.VMEM((3, XR, Z), f32),
            pltpu.VMEM((2, 1, X, Z), f32), pltpu.VMEM((2, 3, XR, Z), f32), pltpu.VMEM((2, 1, XR, Z), f32), pltpu.VMEM((2, 3, XR, Z), f32),
            pltpu.SemaphoreType.DMA((52,)), pltpu.SemaphoreType.DMA((52,)),
            pltpu.SemaphoreType.DMA((ny,)), pltpu.SemaphoreType.DMA((ny,)), pltpu.SemaphoreType.DMA,
        ],
        compiler_params=pltpu.CompilerParams(
            collective_id=0, has_side_effects=True, vmem_limit_bytes=60 * 1024 * 1024),
    )(phase.reshape(X * Y, Z), perm_scale.reshape(X * Y, Z), magnetization.reshape(3, X * Y, Z), stiffness)
    return result.reshape(6, X, Y, Z)


def solution(mesh):
    placed = (
        P("gx", "gy", "gz"),
        P("gx", "gy", "gz"),
        P(None, "gx", "gy", "gz"),
        P(("gx", "gy"), None, "gz"),
    )
    return jax.shard_map(
        per_device, mesh=mesh, in_specs=placed, out_specs=P(None, "gx", "gy", "gz"), check_vma=False
    )
```

```python
import functools
import math

import jax
import jax.numpy as jnp
from jax import lax
from jax.experimental import pallas as pl
from jax.experimental.pallas import tpu as pltpu
from jax.sharding import PartitionSpec as P

SWEEPS = 3
STRAIN_PAIRS = ((0, 0), (1, 1), (2, 2), (0, 1), (1, 2), (0, 2))
STRESS_AT = {(0, 0): 0, (1, 1): 1, (2, 2): 2, (0, 1): 3, (1, 0): 3, (1, 2): 4, (2, 1): 4, (0, 2): 5, (2, 0): 5}
MAGNETO = 4.0
MESH = pl.DeviceIdType.MESH
RIM = 4


def chebyshev_weights(middle, radius, count):
    return [
        1.0 / (middle + radius * math.cos((2 * counter + 1) * math.pi / (2 * count)))
        for counter in range(count)
    ]


def shift(value, dimension, step):
    size = value.shape[dimension]
    return pltpu.roll(value, (-step) % size, dimension)


def sides(value, dimension):
    return shift(value, dimension, 1), shift(value, dimension, -1)


def kernel(sizes, phase_in, perm_in, magnet_in, stiff, out, phase, perm, magnet, in_sem, flat, diag, mom, src, pot1, pot2, stress, load, disp1, disp2,
           mask, modulus, rx_m, rx_s, rx_g, tz_a, tz_m, tz_s, tz_g, rz_a, rz_m, rz_s, rz_g, send_sem, recv_sem, g_send, g_recv, g_local):
    nx, ny, nz, X, Y, Z = sizes
    XR, ZR = X + 2 * RIM, 2 * Z
    gx, gy, gz = lax.axis_index("gx"), lax.axis_index("gy"), lax.axis_index("gz")
    place = {"gx": gx, "gy": gy, "gz": gz}
    count = {"gx": nx, "gy": ny, "gz": nz}

    fetches = [pltpu.make_async_copy(a, b, in_sem.at[i]) for i, (a, b) in enumerate(
        ((magnet_in, magnet), (phase_in, phase), (perm_in, perm)))]
    for fetch in fetches:
        fetch.start()

    def has(axis, side):
        return place[axis] > 0 if side == 0 else place[axis] < count[axis] - 1

    def device(axis, index):
        at = dict(place)
        at[axis] = index
        return (at["gx"], at["gy"], at["gz"])

    def exists(step):
        there = None
        for axis, move in zip(("gx", "gy", "gz"), step):
            if move:
                this = has(axis, 0 if move < 0 else 1)
                there = this if there is None else there & this
        return there

    def beside(step):
        return (gx + step[0], gy + step[1], gz + step[2])

    barrier = pltpu.get_barrier_semaphore()
    greeted = 0
    diagonals = [(dx, dy, 0) for dx in (-1, 1) for dy in (-1, 1)]
    for step in [(-1, 0, 0), (1, 0, 0), (0, 0, -1), (0, 0, 1)] + diagonals:
        @pl.when(exists(step))
        def _():
            pl.semaphore_signal(barrier, inc=1, device_id=beside(step), device_id_type=MESH)
        greeted = greeted + exists(step).astype(jnp.int32)
    for k in range(1, ny):
        pl.semaphore_signal(barrier, inc=1, device_id=device("gy", lax.rem(gy + k, ny)), device_id_type=MESH)
    greeted = greeted + (ny - 1)

    row = lax.broadcasted_iota(jnp.int32, (XR, ZR), 0)
    lane = lax.broadcasted_iota(jnp.int32, (XR, ZR), 1)
    real = ((row < X) | ((row < X + RIM) & has("gx", 1)) | ((row >= X + RIM) & has("gx", 0))) & (
        (lane < Z) | ((lane < Z + Z // 2) & has("gz", 1)) | ((lane >= Z + Z // 2) & has("gz", 0)))
    mask[...] = jnp.where(real, 1.0, 0.0)

    for fetch in fetches:
        fetch.wait()

    for c in range(3):
        flat[c] = magnet[c].astype(jnp.float32)
    for y in range(Y):
        rows = pl.ds(y, X, stride=Y)
        kind = phase[rows, :]
        magnetic = kind == 0
        mu = jnp.where(magnetic, 4.0, jnp.where(kind == 1, 1.5, 1.0)).astype(jnp.float32) * perm[rows, :]
        diag[y] = 6.0 * mu
        for c in range(3):
            mom[c, RIM + y, 0:X, 0:Z] = jnp.where(magnetic, flat[c, rows, :], 0.0)

    for buffer in (rx_m, rx_s, rx_g):
        for side in (0, 1):
            @pl.when(jnp.logical_not(has("gx", side)))
            def _():
                buffer[side] = jnp.zeros(buffer.shape[1:], jnp.float32)
    for buffer in (rx_m, rx_s, rx_g):
        for side, first in ((0, 0), (1, RIM + Y)):
            @pl.when(jnp.logical_not(has("gy", side)))
            def _():
                for way in (0, 1):
                    for c in range(buffer.shape[1]):
                        buffer[way, c, first:first + RIM] = jnp.zeros((RIM, 2 * RIM, Z), jnp.float32)
    for buffer in (rz_a, rz_m, rz_s, rz_g):
        for side in (0, 1):
            @pl.when(jnp.logical_not(has("gz", side)))
            def _():
                buffer[side] = jnp.zeros(buffer.shape[1:], jnp.float32)
    for buffer in (mom, src, load):
        for side, first in ((0, 0), (1, RIM + Y)):
            @pl.when(jnp.logical_not(has("gy", side)))
            def _():
                for c in range(3 if buffer is not src else 1):
                    buffer[c, first:first + RIM] = jnp.zeros((RIM, XR, ZR), jnp.float32)

    pl.semaphore_wait(barrier, greeted)

    def copy_of(piece, number):
        step, source, target = piece
        return pltpu.make_async_remote_copy(
            src_ref=source, dst_ref=target, send_sem=send_sem.at[number], recv_sem=recv_sem.at[number],
            device_id=beside(step), device_id_type=MESH)

    def begin(pieces, base):
        for number, piece in enumerate(pieces):
            @pl.when(exists(piece[0]))
            def _():
                copy_of(piece, base + number).start()

    def finish(pieces, base):
        for number, piece in enumerate(pieces):
            @pl.when(exists(piece[0]))
            def _():
                copy_of(piece, base + number).wait_send()
            @pl.when(exists([-move for move in piece[0]]))
            def _():
                copy_of(piece, base + number).wait_recv()

    def flat_pieces(buffer, width, rx, parts=slice(None)):
        planes = {-1: slice(RIM, RIM + width), 0: slice(RIM, RIM + Y), 1: slice(RIM + Y - width, RIM + Y)}
        landing = {-1: slice(RIM + Y, RIM + Y + width), 0: slice(RIM, RIM + Y), 1: slice(RIM - width, RIM)}
        rows = {-1: slice(0, 2 * RIM), 1: slice(X - 2 * RIM, X)}
        pieces = []
        for dy in (-1, 1):
            pieces.append(((0, dy, 0), buffer.at[parts, planes[dy], 0:X, 0:Z], buffer.at[parts, landing[dy], 0:X, 0:Z]))
        for dy in (0, -1, 1):
            for dx in (-1, 1):
                pieces.append(((dx, dy, 0), buffer.at[parts, planes[dy], rows[dx], 0:Z],
                               rx.at[1 if dx < 0 else 0, parts, landing[dy]]))
        return pieces

    def place_rows(buffer, components, width, rx):
        upper = lax.broadcasted_iota(jnp.int32, (Y + 2 * width, 2 * RIM, Z), 1) < RIM
        span = slice(RIM - width, RIM + Y + width)
        for c in components:
            buffer[c, span, X:XR, 0:Z] = jnp.where(upper, rx[1, c, span], rx[0, c, span])

    block = lax.rem(lax.broadcasted_iota(jnp.int32, (XR, Z), 1) + RIM, Z) // (2 * RIM)
    from_after = lax.rem(lax.broadcasted_iota(jnp.int32, (XR, Z), 1), 2 * RIM) < RIM

    def pack(buffer, components, width, rows, tz, first=0):
        for at, c in enumerate(components, first):
            packed = jnp.zeros((rows, Z), jnp.float32)
            for y in range(RIM - width, RIM + Y + width):
                packed = jnp.where(
                    block[0:rows] == y, pltpu.roll(buffer[c, y, 0:rows, 0:Z], (2 * RIM * y) % Z, 1), packed)
            tz[at] = packed

    def unpack(buffer, components, width, rows, rz, first=0):
        for at, c in enumerate(components, first):
            both = jnp.where(from_after[0:rows], rz[1, at], rz[0, at])
            for y in range(RIM - width, RIM + Y + width):
                buffer[c, y, 0:rows, Z:ZR] = pltpu.roll(both, (-2 * RIM * y) % Z, 1)

    def deep_pieces(tz, rz, parts=slice(None)):
        return [((0, 0, -1), tz.at[parts], rz.at[1, parts]), ((0, 0, 1), tz.at[parts], rz.at[0, parts])]

    def clear_outside(buffer, parts):
        for side, first in ((0, 0), (1, RIM + Y)):
            @pl.when(jnp.logical_not(has("gy", side)))
            def _():
                for c in range(parts):
                    buffer[c, first:first + RIM] = jnp.zeros((RIM, XR, ZR), jnp.float32)

    flat_m = flat_pieces(mom, 1, rx_m)
    deep_a = deep_pieces(tz_a, rz_a)
    begin(flat_m, 0)
    pack(mom, (2,), 0, X, tz_a)
    begin(deep_a, 8)
    finish(flat_m, 0)
    place_rows(mom, (0, 1, 2), 1, rx_m)
    finish(deep_a, 8)
    unpack(mom, (2,), 0, X, rz_a)

    @pl.loop(RIM, RIM + Y, unroll=4)
    def _(y):
        xp, xm = sides(mom[0, y], 0)
        zp, zm = sides(mom[2, y], 1)
        total = (xp - xm) + (mom[1, y + 1] - mom[1, y - 1]) + (zp - zm)
        src[0, y, 0:X, 0:Z] = -0.5 * total[0:X, 0:Z] / diag[y - RIM]

    flat_s = flat_pieces(src, 4, rx_s)
    deep_s = deep_pieces(tz_s, rz_s)
    deep_m = deep_pieces(tz_m, rz_m)
    begin(flat_s, 10)
    pack(mom, (0, 1, 2), 1, XR, tz_m)
    begin(deep_m, 18)
    finish(flat_s, 10)
    place_rows(src, (0,), 4, rx_s)
    pack(src, (0,), 4, XR, tz_s)
    begin(deep_s, 20)

    span = X // ny
    for k in range(1, ny):
        peer = lax.rem(gy + k, ny)
        pltpu.make_async_remote_copy(
            src_ref=stiff.at[:, pl.ds(pl.multiple_of(peer * Y, Y), Y), :],
            dst_ref=modulus.at[pl.ds(gy * span, span)],
            send_sem=g_send.at[k], recv_sem=g_recv.at[k],
            device_id=device("gy", peer), device_id_type=MESH).start()
    own = pltpu.make_async_copy(
        stiff.at[:, pl.ds(pl.multiple_of(gy * Y, Y), Y), :], modulus.at[pl.ds(gy * span, span)], g_local)
    own.start()

    finish(deep_s, 20)
    unpack(src, (0,), 4, XR, rz_s)
    w = chebyshev_weights(1.0, 0.9, SWEEPS)

    def neighbours(buffer, y):
        xp, xm = sides(buffer[0, y], 0)
        zp, zm = sides(buffer[0, y], 1)
        return xp + xm + buffer[0, y + 1] + buffer[0, y - 1] + zp + zm

    @pl.loop(1, 2 * RIM + Y - 1, unroll=2)
    def _(y):
        pot1[0, y] = mask[...] * ((w[0] + w[1] - w[0] * w[1]) * src[0, y] + (w[0] * w[1] / 6.0) * neighbours(src, y))

    clear_outside(pot1, 1)

    @pl.loop(2, 2 * RIM + Y - 2, unroll=4)
    def _(y):
        center = pot1[0, y]
        pot2[0, y] = mask[...] * (center + w[2] * (src[0, y] - center + neighbours(pot1, y) * (1.0 / 6.0)))

    clear_outside(pot2, 1)

    finish(deep_m, 18)
    unpack(mom, (0, 1, 2), 1, XR, rz_m)

    @pl.loop(RIM - 1, RIM + Y + 1, unroll=2)
    def _(y):
        center = pot2[0, y]
        xp, xm = sides(center, 0)
        zp, zm = sides(center, 1)
        m = [mom[c, y] for c in range(3)]
        grad = [xp - xm, pot2[0, y + 1] - pot2[0, y - 1], zp - zm]
        total = [m[c] - 0.5 * grad[c] for c in range(3)]
        inner = (m[0] * total[0] + m[1] * total[1] + m[2] * total[2]) / 3.0
        for number, (a, b) in enumerate(STRAIN_PAIRS):
            if a == b:
                value = MAGNETO * (m[a] * total[a] - inner)
            else:
                value = (0.5 * MAGNETO) * (m[a] * total[b] + m[b] * total[a])
            stress[number, y] = value

    for k in range(1, ny):
        peer = lax.rem(gy + k, ny)
        copy = pltpu.make_async_remote_copy(
            src_ref=stiff.at[:, pl.ds(pl.multiple_of(peer * Y, Y), Y), :],
            dst_ref=modulus.at[pl.ds(lax.rem(gy + ny - k, ny) * span, span)],
            send_sem=g_send.at[k], recv_sem=g_recv.at[k],
            device_id=device("gy", peer), device_id_type=MESH)
        copy.wait_send()
        copy.wait_recv()
    own.wait()
    for y in range(Y):
        diag[y] = 8.0 * modulus.reshape(X * Y, Z)[pl.ds(y, X, stride=Y), :]

    flat_g = [flat_pieces(load, 3, rx_g, slice(a, a + 1)) for a in range(3)]
    deep_g = [deep_pieces(tz_g, rz_g, slice(a, a + 1)) for a in range(3)]
    for a in range(3):
        @pl.loop(RIM, RIM + Y, unroll=4)
        def _(y):
            xp, xm = sides(stress[STRESS_AT[a, 0], y], 0)
            zp, zm = sides(stress[STRESS_AT[a, 2], y], 1)
            n = STRESS_AT[a, 1]
            force = 0.5 * ((xp - xm) + (stress[n, y + 1] - stress[n, y - 1]) + (zp - zm))[0:X, 0:Z]
            load[a, y, 0:X, 0:Z] = force.astype(jnp.bfloat16).astype(jnp.float32) / diag[y - RIM]

        begin(flat_g[a], 22 + 10 * a)
    for a in range(3):
        finish(flat_g[a], 22 + 10 * a)
        place_rows(load, (a,), 3, rx_g)
        pack(load, (a,), 3, XR, tz_g, a)
        begin(deep_g[a], 30 + 10 * a)
    for a in range(3):
        finish(deep_g[a], 30 + 10 * a)
        unpack(load, (a,), 3, XR, rz_g, a)
    v = chebyshev_weights(1.3, 1.2, SWEEPS)

    def navier(buffer, y):
        u = [buffer[c, y] for c in range(3)]
        up = [buffer[c, y + 1] for c in range(3)]
        um = [buffer[c, y - 1] for c in range(3)]
        xs = [sides(u[c], 0) for c in range(3)]
        zs = [sides(u[c], 1) for c in range(3)]
        dy = [up[c] - um[c] for c in range(3)]
        dx0 = xs[0][0] - xs[0][1]
        dz2 = zs[2][0] - zs[2][1]
        ap, am = sides(dy[1] + dz2, 0)
        bp, bm = sides(dy[0], 0)
        cp, cm = sides(dy[2], 1)
        ep, em = sides(dx0 + dy[1], 1)
        mixed = [ap - am, (bp - bm) + (cp - cm), ep - em]
        result = []
        for c in range(3):
            along = [xs[c][0] + xs[c][1], up[c] + um[c], zs[c][0] + zs[c][1]]
            rest = along[0] + along[1] + along[2] + along[c]
            result.append(8.0 * u[c] - rest - 0.25 * mixed[c])
        return u, result

    @pl.loop(2, 2 * RIM + Y - 2, unroll=4)
    def _(y):
        u, result = navier(load, y)
        for c in range(3):
            disp1[c, y] = mask[...] * ((v[0] + v[1]) * u[c] - (v[0] * v[1] / 8.0) * result[c])

    clear_outside(disp1, 3)

    @pl.loop(3, 2 * RIM + Y - 3, unroll=2)
    def _(y):
        u, result = navier(disp1, y)
        for c in range(3):
            disp2[c, y] = mask[...] * (u[c] + v[2] * (load[c, y] - 0.125 * result[c]))

    clear_outside(disp2, 3)

    for y in range(RIM, RIM + Y):
        rows = pl.ds(y - RIM, X, stride=Y)
        gradient = {}
        for c in range(3):
            u = disp2[c, y]
            xp, xm = sides(u, 0)
            zp, zm = sides(u, 1)
            gradient[c, 0] = (xp - xm)[0:X, 0:Z]
            gradient[c, 1] = (disp2[c, y + 1] - disp2[c, y - 1])[0:X, 0:Z]
            gradient[c, 2] = (zp - zm)[0:X, 0:Z]
        for number, (a, b) in enumerate(STRAIN_PAIRS):
            flat[number, rows, :] = 0.25 * (gradient[b, a] + gradient[a, b])
    for number in range(6):
        out[number] = flat[number].astype(jnp.bfloat16)


def per_device(phase, perm_scale, magnetization, stiffness):
    X, Y, Z = phase.shape
    nx, ny, nz = (lax.axis_size(axis) for axis in ("gx", "gy", "gz"))
    XR, ZR, P2 = X + 2 * RIM, 2 * Z, Y + 2 * RIM
    f32 = jnp.float32
    field = lambda parts: pltpu.VMEM((parts, P2, XR, ZR), f32)
    rx = lambda parts: pltpu.VMEM((2, parts, P2, 2 * RIM, Z), f32)
    vmem = pl.BlockSpec(memory_space=pltpu.VMEM)
    result = pl.pallas_call(
        functools.partial(kernel, (nx, ny, nz, X, Y, Z)),
        out_shape=jax.ShapeDtypeStruct((6, X * Y, Z), jnp.bfloat16),
        in_specs=[pl.BlockSpec(memory_space=pl.ANY)] * 4,
        out_specs=vmem,
        scratch_shapes=[
            pltpu.VMEM((X * Y, Z), jnp.int32), pltpu.VMEM((X * Y, Z), f32), pltpu.VMEM((3, X * Y, Z), jnp.bfloat16),
            pltpu.SemaphoreType.DMA((3,)),
            pltpu.VMEM((6, X * Y, Z), f32), pltpu.VMEM((Y, X, Z), f32),
            field(3), field(1), field(1), field(1), field(6), field(3), field(3), field(3),
            pltpu.VMEM((XR, ZR), f32), pltpu.VMEM((X, Y, Z), f32),
            rx(3), rx(1), rx(3),
            pltpu.VMEM((1, X, Z), f32), pltpu.VMEM((3, XR, Z), f32), pltpu.VMEM((1, XR, Z), f32), pltpu.VMEM((3, XR, Z), f32),
            pltpu.VMEM((2, 1, X, Z), f32), pltpu.VMEM((2, 3, XR, Z), f32), pltpu.VMEM((2, 1, XR, Z), f32), pltpu.VMEM((2, 3, XR, Z), f32),
            pltpu.SemaphoreType.DMA((52,)), pltpu.SemaphoreType.DMA((52,)),
            pltpu.SemaphoreType.DMA((ny,)), pltpu.SemaphoreType.DMA((ny,)), pltpu.SemaphoreType.DMA,
        ],
        compiler_params=pltpu.CompilerParams(
            collective_id=0, has_side_effects=True, vmem_limit_bytes=60 * 1024 * 1024),
    )(phase.reshape(X * Y, Z), perm_scale.reshape(X * Y, Z), magnetization.reshape(3, X * Y, Z), stiffness)
    return result.reshape(6, X, Y, Z)


def solution(mesh):
    placed = (
        P("gx", "gy", "gz"),
        P("gx", "gy", "gz"),
        P(None, "gx", "gy", "gz"),
        P(("gx", "gy"), None, "gz"),
    )
    return jax.shard_map(
        per_device, mesh=mesh, in_specs=placed, out_specs=P(None, "gx", "gy", "gz"), check_vma=False
    )
```
